256 devices in a mesh: prefix: 32 (over z, y_lo, core), branch: 8 (over y_hi, x).
Axes of the slice: x: 4, y: 4 (y_hi: 2, y_lo: 2; y = y_hi * 2 + y_lo), z: 8, core: 2. Of those that a mesh axis runs over, the one named last changes fastest.
Arguments:
- queries: bfloat16 [32, 8, 256, 4096], P('prefix', 'branch'), may hold values from -5 to 5
- branch_kv: bfloat16 [32, 8, 2, 256, 512], P('prefix', 'branch'), may hold values from -5 to 5
- prefix_kv: bfloat16 [32, 2, 512, 512], P('prefix', None, 'branch'), may hold values from -6 to 6
- out_grad: bfloat16 [32, 8, 256, 4096], P('prefix', 'branch'), may hold values from -6 to 6
- value_weight: float32 [4096], replicated, may hold values from -1.5 to 1.5
- value_grad: float32 [32, 8, 256], P('prefix', 'branch'), may hold values from -6 to 6
- parents: int32 [32], replicated, may hold values from 0 to 31
- lengths: int32 [32, 8], P('prefix', 'branch'), may hold values from 128 to 256, as said below
Outputs:
- values: float32 [32, 8, 256], P('prefix', 'branch')
- query_grad: bfloat16 [32, 8, 256, 4096], P('prefix', 'branch')
- branch_kv_grad: bfloat16 [32, 8, 2, 256, 512], P('prefix', 'branch')
- prefix_kv_grad: float32 [32, 2, 512, 512], P('prefix', None, 'branch')
The draws below stay inside these ranges and needn't reach their ends.
Inputs may be any that keep to these rules, and one draw needn't show every extreme that they name: `lengths`: each length is a multiple of 128; some branch has 256.
All inputs are finite; a program needn't handle non-finite values.
Results may differ from the reference program's by a relative error of at most 0.0092.
Values may be sent and summed in bfloat16 or wider, within the bound.
No kernel may reach another device: no remote copies, remote signals or barrier semaphores. Data moves between devices by JAX's collectives and lax.ppermute only.
A program may use at most 64 MiB of HBM per device.

```python
import math
import jax
import jax.numpy as jnp
import numpy as np
from jax import lax

QH = 32
KVH = 4
HD = 128
BLOCK = 128
BLEN = 256
PLEN = 512
GROUPS = 32
BRANCHES = 8


def draw_queries(key, part):
    key = jax.random.fold_in(key, 11)
    full_shape = (GROUPS, BRANCHES, BLEN, QH * HD)
    drawn = jnp.clip(jax.random.normal(key, full_shape, jnp.float32), -5.0, 5.0)
    return drawn.astype(jnp.bfloat16)


def draw_branch_kv(key, part):
    key = jax.random.fold_in(key, 17)
    full_shape = (GROUPS, BRANCHES, 2, BLEN, KVH * HD)
    drawn = jnp.clip(jax.random.normal(key, full_shape, jnp.float32), -5.0, 5.0)
    return drawn.astype(jnp.bfloat16)


def draw_lengths(key, part):
    key = jax.random.fold_in(key, 29)
    length_key, spot_key = jax.random.split(key)
    most_blocks = BLEN // BLOCK
    blocks = jax.random.randint(length_key, (GROUPS, BRANCHES), 1, most_blocks + 1)
    forced_spot = jax.random.randint(spot_key, (), 0, GROUPS * BRANCHES)
    position = jnp.arange(GROUPS * BRANCHES).reshape(GROUPS, BRANCHES)
    blocks = jnp.where(position == forced_spot, most_blocks, blocks)
    return (blocks * BLOCK).astype(jnp.int32)


def with_ends(values, key, smallest, top_value):
    longest = values.shape.index(max(values.shape))
    spots = []
    for shift in (0, 1):
        where = [jax.random.randint(jax.random.fold_in(key, axis), (), 0, length) for axis, length in enumerate(values.shape)]
        where[longest] = (where[longest] + shift) % values.shape[longest]
        spots.append(tuple(where))
    return values.at[spots[0]].set(smallest).at[spots[1]].set(top_value)


def levels(rng, shape, pieces, smallest, top_value):
    level = 1.0
    for axis_at, shards_of in pieces:
        draws = jax.random.uniform(jax.random.fold_in(jax.random.fold_in(rng, 6), axis_at), (shards_of,), jnp.float32, smallest / len(pieces), top_value / len(pieces))
        level = level * jnp.repeat(jnp.exp(draws), shape[axis_at] // shards_of).reshape((-1,) + (1,) * (len(shape) - 1 - axis_at))
    return level


def rank_table(amount, lean):
    portions = [(1 << 20) // math.isqrt(grade ** lean) + 1 for grade in range(1, amount + 1)]
    spread = 1 + sum(portions) // (1 << 30)
    return np.cumsum(np.array([max(1, weight // spread) for weight in portions]))


def skewed_ids(own_key, extent, number_of, skew):
    grid = rank_table(number_of, skew)
    pick = jax.random.randint(jax.random.fold_in(own_key, 1), extent, 0, int(grid[number_of - 1]))
    standing = jnp.searchsorted(jnp.asarray(grid, jnp.int32), pick, side="right")
    return jax.random.permutation(jax.random.fold_in(own_key, 2), number_of)[standing].astype(jnp.int32)


def bell_draw(key, shape, deviation, limit, cuts=(), kind=jnp.bfloat16):
    array = jax.random.normal(key, shape, jnp.float32) * deviation
    if len(cuts) > 0:
        array = levels(key, shape, cuts, -0.22, 0.18) * array
    return jnp.clip(array, min=-limit, max=limit).astype(kind)


def setup_inputs(seed: int = 0) -> dict:
    keys = jax.random.split(jax.random.key(seed), 9)
    queries = draw_queries(jax.random.fold_in(keys[8], 71), 0)
    branch_kv = draw_branch_kv(jax.random.fold_in(keys[8], 71), 0)
    prefix_kv = bell_draw(keys[2], (GROUPS, 2, PLEN, KVH * HD), 1.0, 6.0, ((0, 32), (2, 8)))
    out_grad = bell_draw(keys[3], (GROUPS, BRANCHES, BLEN, QH * HD), 1.0, 6.0, ((0, 32), (1, 8)))
    value_weight = bell_draw(keys[4], (QH * HD,), 0.25, 1.5, (), jnp.float32)
    value_grad = bell_draw(keys[5], (GROUPS, BRANCHES, BLEN), 1.0, 6.0, ((0, 32), (1, 8)), jnp.float32)
    parents = with_ends(skewed_ids(keys[6], (GROUPS,), GROUPS, 2), jax.random.fold_in(keys[6], 3), 0, GROUPS - 1).astype(jnp.int32)
    lengths = draw_lengths(jax.random.fold_in(keys[8], 71), 0)
    return dict(queries=queries, branch_kv=branch_kv, prefix_kv=prefix_kv, out_grad=out_grad, value_weight=value_weight, value_grad=value_grad, parents=parents, lengths=lengths)


NEG_FILL = -1.0e30


def branch_pass(query_block, branch_pair, prefix_pair, upper_cot, value_weight, value_cot, live_len):
    head_ratio = QH // KVH
    score_scale = HD ** -0.5
    query_len = query_block.shape[0]
    prefix_len = prefix_pair.shape[1]
    key_rows = jnp.concatenate([prefix_pair[0], branch_pair[0]], axis=0).astype(jnp.float32)
    value_rows = jnp.concatenate([prefix_pair[1], branch_pair[1]], axis=0).astype(jnp.float32)
    key_count = key_rows.shape[0]
    key_rows = key_rows.reshape(key_count, KVH, HD)
    value_rows = value_rows.reshape(key_count, KVH, HD)
    query_heads = query_block.astype(jnp.float32).reshape(query_len, KVH, head_ratio, HD)
    row_index = lax.broadcasted_iota(jnp.int32, (query_len, key_count), 0)
    col_index = lax.broadcasted_iota(jnp.int32, (query_len, key_count), 1)
    allowed = (col_index < prefix_len) | (col_index - prefix_len <= row_index)
    live_rows = lax.broadcasted_iota(jnp.int32, (query_len, 1), 0) < live_len
    scores = jnp.einsum("tkrd,skd->krts", query_heads, key_rows) * score_scale
    scores = jnp.where(allowed, scores, NEG_FILL)
    row_max = jnp.max(scores, axis=3, keepdims=True)
    shifted = jnp.exp(scores - row_max)
    weights = shifted / jnp.sum(shifted, axis=3, keepdims=True)
    weights = jnp.where(live_rows, weights, 0.0)
    weights_low = lax.optimization_barrier(weights.astype(jnp.bfloat16)).astype(jnp.float32)
    attended = jnp.einsum("krts,skd->tkrd", weights_low, value_rows)
    weight_heads = value_weight.reshape(KVH, head_ratio, HD)
    values = jnp.sum(attended * weight_heads[None], axis=(1, 2, 3))
    out_cot = upper_cot.astype(jnp.float32) + value_cot[:, None] * value_weight[None, :]
    out_cot = lax.optimization_barrier(out_cot.astype(jnp.bfloat16)).astype(jnp.float32)
    out_cot = out_cot.reshape(query_len, KVH, head_ratio, HD)
    value_piece = jnp.einsum("krts,tkrd->skd", weights_low, out_cot)
    prob_grad = jnp.einsum("tkrd,skd->krts", out_cot, value_rows)
    row_delta = jnp.transpose(jnp.sum(out_cot * attended, axis=3), (1, 2, 0))
    score_grad = weights * (prob_grad - row_delta[..., None])
    score_low = lax.optimization_barrier(score_grad.astype(jnp.bfloat16)).astype(jnp.float32)
    query_grad = (jnp.einsum("krts,skd->tkrd", score_low, key_rows) * score_scale).astype(jnp.bfloat16)
    key_piece = jnp.einsum("krts,tkrd->skd", score_low, query_heads) * score_scale
    paired = jnp.stack([key_piece, value_piece]).reshape(2, key_count, KVH * HD)
    return (values, query_grad.reshape(query_len, QH * HD),
            paired[:, prefix_len:].astype(jnp.bfloat16), paired[:, :prefix_len])


def reference(queries, branch_kv, prefix_kv, out_grad, value_weight, value_grad, parents, lengths):
    def group_step(grad_total, group_index):
        parent = parents[group_index]
        prefix_pair = prefix_kv[parent]

        def one_branch(query_block, branch_pair, upper_cot, value_cot, live_len):
            return branch_pass(query_block, branch_pair, prefix_pair, upper_cot, value_weight, value_cot, live_len)

        values, query_grad, branch_grad, prefix_grad = jax.vmap(one_branch)(
            queries[group_index], branch_kv[group_index], out_grad[group_index],
            value_grad[group_index], lengths[group_index])
        grad_total = grad_total.at[parent].add(jnp.sum(prefix_grad, axis=0))
        return grad_total, (values, query_grad, branch_grad)

    start_total = jnp.zeros(prefix_kv.shape, jnp.float32)
    grad_total, (values, query_grad, branch_grad) = lax.scan(
        group_step, start_total, jnp.arange(GROUPS, dtype=jnp.int32))
    return values, query_grad, branch_grad, grad_total
```

```python
import functools
import jax
import jax.numpy as jnp
from jax import lax
from jax.experimental import pallas as pl
from jax.experimental.pallas import tpu as pltpu
from jax.sharding import Mesh, PartitionSpec as P
QH=32;KVH=4;HD=128;RATIO=8
LOG2E=1.4426950408889634
F32=jnp.float32; BF=jnp.bfloat16

def attn_kernel(len_ref, q_ref, og_ref, vw_ref, vg_ref, bkv_ref, *rest, npieces, plen, unroll):
    pieces=rest[:npieces]
    dq_ref, bg_ref, val_ref = rest[npieces:npieces+3]
    pg = rest[npieces+3:npieces+3+npieces]
    k_s, v_s, kt_s, vt_s, dk_s, dv_s, val_s = rest[npieces+3+npieces:]
    j=pl.program_id(0)
    T=q_ref.shape[0]
    rows=plen//npieces
    S=plen+T
    for i in range(npieces):
        k_s[i*rows:(i+1)*rows,:]=pieces[i][0]
        v_s[i*rows:(i+1)*rows,:]=pieces[i][1]
    k_s[plen:,:]=bkv_ref[0]
    v_s[plen:,:]=bkv_ref[1]
    kt_s[...]=k_s[...].T
    vt_s[...]=v_s[...].T
    dk_s[...]=jnp.zeros_like(dk_s)
    dv_s[...]=jnp.zeros_like(dv_s)
    vg_col=jnp.broadcast_to(vg_ref[...],(8,T)).T[:,:1]
    live=(lax.broadcasted_iota(jnp.int32,(1,T),1)<len_ref[0]).astype(F32)
    key_i=lax.broadcasted_iota(jnp.int32,(T,T),0)
    row_i=lax.broadcasted_iota(jnp.int32,(T,T),1)
    allowed=key_i<=row_i
    scale=HD**-0.5
    @pl.when(j==0)
    def _():
        val_s[...]=jnp.zeros_like(val_s)
    def head(h,_):
        cols=pl.ds(pl.multiple_of(h*HD,HD),HD)
        q=q_ref[:,cols]
        vw=vw_ref[:,cols]
        c=(og_ref[:,cols].astype(F32)+vg_col*vw).astype(BF)
        ct=c.T
        s=lax.dot_general(k_s[...],q,(((1,),(1,)),((),())),preferred_element_type=F32)
        sp=s[:plen]*(scale*LOG2E)
        sb=jnp.where(allowed,s[plen:]*(scale*LOG2E),-1e30)
        m=jnp.maximum(jnp.max(sp,axis=0,keepdims=True),jnp.max(sb,axis=0,keepdims=True))
        pp=jnp.exp2(sp-m); pb=jnp.exp2(sb-m)
        l=jnp.sum(pp,axis=0,keepdims=True)+jnp.sum(pb,axis=0,keepdims=True)
        rl=live/l
        w=jnp.concatenate([pp*rl,pb*rl],axis=0)
        wl=w.astype(BF)
        att=jnp.dot(vt_s[...],wl,preferred_element_type=F32)
        dp=jnp.dot(v_s[...],ct,preferred_element_type=F32)
        delta=jnp.sum(ct.astype(F32)*att,axis=0,keepdims=True)
        val_s[...]+=att*jnp.broadcast_to(vw,(8,HD)).T[:,:1]
        ds=(w*(dp-delta)).astype(BF)
        dq=jnp.dot(kt_s[...],ds,preferred_element_type=F32)*scale
        dq_ref[:,cols]=dq.T.astype(BF)
        dv_s[...]+=jnp.dot(wl,c,preferred_element_type=F32)
        dk_s[...]+=jnp.dot(ds,q,preferred_element_type=F32)
        return 0
    lax.fori_loop(0,RATIO,head,0,unroll=unroll)
    dk=dk_s[...]*scale
    dv=dv_s[...]
    for i in range(npieces):
        pg[i][0]=dk[i*rows:(i+1)*rows].astype(BF)
        pg[i][1]=dv[i*rows:(i+1)*rows].astype(BF)
    bg_ref[0]=dk[plen:].astype(BF)
    bg_ref[1]=dv[plen:].astype(BF)
    @pl.when(j==pl.num_programs(0)-1)
    def _():
        val_ref[...]=jnp.sum(val_s[...],axis=0,keepdims=True)

def attn(lengths,q,og,vw,vg,bkv,pieces,unroll=1):
    T=q.shape[0]; n=len(pieces); rows=pieces[0].shape[1]; plen=rows*n; S=plen+T
    W=RATIO*HD
    col=lambda j:(0,j)
    in_specs=[pl.BlockSpec(memory_space=pltpu.SMEM),
      pl.BlockSpec((T,W),col),pl.BlockSpec((T,W),col),pl.BlockSpec((1,W),col),
      pl.BlockSpec((1,T),lambda j:(0,0)),
      pl.BlockSpec((2,T,HD),lambda j:(0,0,j))]+[pl.BlockSpec((2,rows,HD),lambda j:(0,0,j))]*n
    out_specs=[pl.BlockSpec((T,W),col),pl.BlockSpec((2,T,HD),lambda j:(0,0,j)),pl.BlockSpec((1,T),lambda j:(0,0))]+[pl.BlockSpec((2,rows,HD),lambda j:(0,0,j))]*n
    out_shape=[jax.ShapeDtypeStruct((T,QH*HD),BF),jax.ShapeDtypeStruct((2,T,KVH*HD),BF),jax.ShapeDtypeStruct((1,T),F32)]+[jax.ShapeDtypeStruct((2,rows,KVH*HD),BF)]*n
    return pl.pallas_call(functools.partial(attn_kernel,npieces=n,plen=plen,unroll=unroll),grid=(KVH,),
      in_specs=in_specs,out_specs=out_specs,out_shape=out_shape,
      scratch_shapes=[pltpu.VMEM((S,HD),BF),pltpu.VMEM((S,HD),BF),pltpu.VMEM((HD,S),BF),pltpu.VMEM((HD,S),BF),
        pltpu.VMEM((S,HD),F32),pltpu.VMEM((S,HD),F32),pltpu.VMEM((HD,T),F32)],
      compiler_params=pltpu.CompilerParams(vmem_limit_bytes=48*1024*1024),
    )(lengths,q,og,vw,vg,bkv,*pieces)


Z, YL, CORE, YH, X = 8, 2, 2, 2, 4


def shift(value, axis, step, size):
    return lax.ppermute(value, axis, [(i, (i + step) % size) for i in range(size)])


def gather_z(value):
    got = {0: value}
    for k in (2, -2, 1, -1):
        got[k % Z] = shift(value, "z", k, Z)
    got[4] = shift(got[2], "z", 2, Z)
    got[3] = shift(got[1], "z", 2, Z)
    got[5] = shift(got[7], "z", -2, Z)
    return [got[k] for k in range(Z)]


def pick(index, options):
    out = options[0]
    for k in range(1, len(options)):
        out = jnp.where(index == k, options[k], out)
    return out


def shards(queries, branch_kv, prefix_kv, out_grad, value_weight, value_grad, parents, lengths):
    my_z, my_yl, my_c = lax.axis_index("z"), lax.axis_index("yl"), lax.axis_index("c")
    pair = my_yl * CORE + my_c

    def parent_of(z, other_pair):
        return lax.dynamic_index_in_dim(parents, z * (YL * CORE) + other_pair, 0, keepdims=False)

    ring = gather_z(prefix_kv[0])
    received = []
    for step in range(YL * CORE):
        wanted = parent_of(my_z, (pair + step) % (YL * CORE))
        sent = pick((my_z - wanted // (YL * CORE)) % Z, ring)
        received.append(shift(sent, ("yl", "c"), step, YL * CORE) if step else sent)
    mine = parent_of(my_z, pair)
    picked = pick((pair - mine % (YL * CORE)) % (YL * CORE), received)

    row = [picked] + [shift(picked, "x", k, X) for k in range(1, X)]
    pieces = row + [shift(piece, "yh", 1, YH) for piece in row]

    query_grad, branch_grad, values, *piece_grads = attn(
        lengths[0], queries[0, 0], out_grad[0, 0], value_weight[None], value_grad[0], branch_kv[0, 0], pieces)

    back = []
    for index, piece in enumerate(piece_grads):
        jy, k = divmod(index, X)
        perm = [(i, ((i // X - jy) % YH) * X + (i % X - k) % X) for i in range(YH * X)]
        back.append(lax.ppermute(piece, ("yh", "x"), perm) if index else piece)
    share = sum(piece.astype(F32) for piece in back).astype(BF)

    ring = gather_z(share)
    owners = [parent_of((my_z - k) % Z, pair) for k in range(Z)]
    received = []
    for step in range(YL * CORE):
        target = (pair + step) % (YL * CORE)
        slot = sum(
            jnp.where(owners[k] == my_z * (YL * CORE) + target, ring[k].astype(F32), 0.0) for k in range(Z))
        received.append(
            shift(slot.astype(BF), ("yl", "c"), step, YL * CORE).astype(F32) if step else slot)
    prefix_grad = sum(received)
    return values[None], query_grad[None, None], branch_grad[None, None], prefix_grad[None]


def solution(mesh):
    fine = Mesh(mesh.devices.reshape(Z, YL, CORE, YH, X), ("z", "yl", "c", "yh", "x"))
    prefix, branch = ("z", "yl", "c"), ("yh", "x")
    in_specs = (
        P(prefix, branch, None, None),
        P(prefix, branch, None, None, None),
        P(prefix, None, branch, None),
        P(prefix, branch, None, None),
        P(),
        P(prefix, branch, None),
        P(),
        P(prefix, branch),
    )
    out_specs = (
        P(prefix, branch, None),
        P(prefix, branch, None, None),
        P(prefix, branch, None, None, None),
        P(prefix, None, branch, None),
    )
    return jax.shard_map(shards, mesh=fine, in_specs=in_specs, out_specs=out_specs, check_vma=False)
```

```python
import functools

import jax
import jax.numpy as jnp
from jax import lax
from jax.experimental import pallas as pl
from jax.experimental.pallas import tpu as pltpu
from jax.sharding import Mesh, PartitionSpec as P

QH = 32
KVH = 4
HD = 128
RATIO = QH // KVH
LOG2E = 1.4426950408889634
SCALE = HD**-0.5
F32 = jnp.float32
BF = jnp.bfloat16
VMEM = 56 * 1024 * 1024
Z, YL, CORE, YH, X = 8, 2, 2, 2, 4
FOUR = YL * CORE


def tn(a, b):
    return lax.dot_general(a, b, (((0,), (0,)), ((), ())), preferred_element_type=F32)


def nt(a, b):
    return lax.dot_general(a, b, (((1,), (1,)), ((), ())), preferred_element_type=F32)


def nn(a, b):
    return jnp.dot(a, b, preferred_element_type=F32)


def load_keys(k_s, v_s, pieces, bkv_ref, plen, rows):
    for i in range(YH * X):
        k_s[i * rows : (i + 1) * rows, :] = pieces[i][0]
        v_s[i * rows : (i + 1) * rows, :] = pieces[i][1]
    k_s[plen:, :] = bkv_ref[0]
    v_s[plen:, :] = bkv_ref[1]


def set_bias(bias_s):
    size = bias_s.shape[0]
    key_at = lax.broadcasted_iota(jnp.int32, (size, size), 0)
    row_at = lax.broadcasted_iota(jnp.int32, (size, size), 1)
    bias_s[...] = jnp.where(key_at <= row_at, 0.0, -1e30)


def column(row, size):
    return jnp.broadcast_to(row, (8, size)).T[:, :1]


def pipeline(stages, count):
    depth = len(stages)
    for step in range(count + depth - 1):
        for late, stage in enumerate(stages):
            if 0 <= step - late < count:
                stage(step - late)


def prefix_kernel(len_ref, q_ref, og_ref, vw_ref, vg_ref, bkv_ref, *rest, plen):
    pieces = rest[: YH * X]
    val_ref, *grads, stat_ref, k_s, v_s, dk_s, dv_s, val_s, bias_s = rest[YH * X :]
    j = pl.program_id(0)
    size = q_ref.shape[0]
    rows = plen // (YH * X)
    load_keys(k_s, v_s, pieces, bkv_ref, plen, rows)
    vg_col = column(vg_ref[...], size)
    live = (lax.broadcasted_iota(jnp.int32, (1, size), 1) < len_ref[0]).astype(F32)

    @pl.when(j == 0)
    def _():
        val_s[...] = jnp.zeros_like(val_s)
        set_bias(bias_s)

    state = {}
    value_sum = [jnp.zeros((size, HD), F32)]

    def softmax_stage(h):
        cols = slice(h * HD, (h + 1) * HD)
        q = q_ref[:, cols]
        cot = (og_ref[:, cols].astype(F32) + vg_col * vw_ref[:, cols]).astype(BF)
        s = nt(k_s[...], q)
        sp = s[:plen] * (SCALE * LOG2E)
        sb = s[plen:] * (SCALE * LOG2E) + bias_s[...]
        top = jnp.maximum(jnp.max(sp, axis=0, keepdims=True), jnp.max(sb, axis=0, keepdims=True))
        pp = jnp.exp2(sp - top)
        pb = jnp.exp2(sb - top)
        total = jnp.sum(pp, axis=0, keepdims=True) + jnp.sum(pb, axis=0, keepdims=True)
        part = live / total
        w = pp * part
        low = jnp.concatenate([w.astype(BF), (pb * part).astype(BF)], axis=0)
        stat_ref[0, h : h + 1, :] = top
        stat_ref[0, RATIO + h : RATIO + h + 1, :] = part
        state[h] = (q, cot, w, low)

    def cot_stage(h):
        q, cot, w, low = state[h]
        att = tn(low, v_s[...])
        dp = nt(v_s[:plen, :], cot)
        delta = jnp.sum((cot.astype(F32) * att).T, axis=0, keepdims=True)
        stat_ref[0, 2 * RATIO + h : 2 * RATIO + h + 1, :] = delta
        value_sum[0] = value_sum[0] + att * vw_ref[:, h * HD : (h + 1) * HD]
        state[h] = (q, cot, w, low, dp, delta)

    def grad_stage(h):
        q, cot, w, low, dp, delta = state.pop(h)
        ds = (w * (dp - delta)).astype(BF)
        dv = nn(low[:plen], cot)
        dk = nn(ds, q)
        if h == 0:
            dv_s[...] = dv
            dk_s[...] = dk
        else:
            dv_s[...] += dv
            dk_s[...] += dk

    pipeline([softmax_stage, cot_stage, grad_stage], RATIO)
    val_s[...] += value_sum[0]
    dk = (dk_s[...] * SCALE).astype(BF)
    dv = dv_s[...].astype(BF)
    for i in range(YH * X):
        grads[i][0] = dk[i * rows : (i + 1) * rows]
        grads[i][1] = dv[i * rows : (i + 1) * rows]

    @pl.when(j == pl.num_programs(0) - 1)
    def _():
        val_ref[...] = jnp.sum(val_s[...].T, axis=0, keepdims=True)


def common_specs(size, rows, at):
    wide = RATIO * HD
    return [
        pl.BlockSpec((size, wide), lambda j: (0, j + at)),
        pl.BlockSpec((size, wide), lambda j: (0, j + at)),
        pl.BlockSpec((1, wide), lambda j: (0, j + at)),
        pl.BlockSpec((1, size), lambda j: (0, 0)),
        pl.BlockSpec((2, size, HD), lambda j: (0, 0, j + at)),
    ] + [pl.BlockSpec((2, rows, HD), lambda j: (0, 0, j + at))] * (YH * X)


def prefix_pass(lengths, q, og, vw, vg, bkv, pieces):
    size, rows = q.shape[0], pieces[0].shape[1]
    plen = YH * X * rows
    grad = jax.ShapeDtypeStruct((2, rows, KVH * HD), BF)
    grad_spec = pl.BlockSpec((2, rows, HD), lambda j: (0, 0, j))
    return pl.pallas_call(
        functools.partial(prefix_kernel, plen=plen),
        grid=(KVH,),
        in_specs=[pl.BlockSpec(memory_space=pltpu.SMEM)] + common_specs(size, rows, 0),
        out_specs=[pl.BlockSpec((1, size), lambda j: (0, 0)), *[grad_spec] * (YH * X),
                   pl.BlockSpec((1, 3 * RATIO, size), lambda j: (j, 0, 0))],
        out_shape=[jax.ShapeDtypeStruct((1, size), F32), *[grad] * (YH * X),
                   jax.ShapeDtypeStruct((KVH, 3 * RATIO, size), F32)],
        scratch_shapes=[
            pltpu.VMEM((plen + size, HD), BF), pltpu.VMEM((plen + size, HD), BF),
            pltpu.VMEM((plen, HD), F32), pltpu.VMEM((plen, HD), F32),
            pltpu.VMEM((size, HD), F32), pltpu.VMEM((size, size), F32)],
        compiler_params=pltpu.CompilerParams(vmem_limit_bytes=VMEM),
        cost_estimate=pl.CostEstimate(flops=6 * 10**9, bytes_accessed=8 * 10**6, transcendentals=6 * 10**6),
    )(lengths, q, og, vw, vg, bkv, *pieces)


def branch_kernel(q_ref, og_ref, vw_ref, vg_ref, bkv_ref, *rest, plen):
    pieces, stat_ref = rest[: YH * X], rest[YH * X]
    dq_ref, bg_ref, done_ref, k_s, v_s, dk_s, dv_s, bias_s = rest[-8:]
    size = q_ref.shape[0]
    rows = plen // (YH * X)
    load_keys(k_s, v_s, pieces, bkv_ref, plen, rows)
    vg_col = column(vg_ref[...], size)
    set_bias(bias_s)
    state = {}

    def weight_stage(h):
        cols = slice(h * HD, (h + 1) * HD)
        q = q_ref[:, cols]
        cot = (og_ref[:, cols].astype(F32) + vg_col * vw_ref[:, cols]).astype(BF)
        s = nt(k_s[...], q)
        top = stat_ref[0, h : h + 1, :]
        part = stat_ref[0, RATIO + h : RATIO + h + 1, :]
        wp = jnp.exp2(s[:plen] * (SCALE * LOG2E) - top) * part
        wb = jnp.exp2(s[plen:] * (SCALE * LOG2E) + bias_s[...] - top) * part
        state[h] = (q, cot, wp, wb)

    def cot_stage(h):
        q, cot, wp, wb = state[h]
        delta = stat_ref[0, 2 * RATIO + h : 2 * RATIO + h + 1, :]
        dp = nt(v_s[...], cot)
        ds = jnp.concatenate([(wp * (dp[:plen] - delta)).astype(BF), (wb * (dp[plen:] - delta)).astype(BF)], axis=0)
        state[h] = (q, cot, wb.astype(BF), ds)

    def grad_stage(h):
        q, cot, low, ds = state.pop(h)
        dq_ref[:, h * HD : (h + 1) * HD] = (tn(ds, k_s[...]) * SCALE).astype(BF)
        dv = nn(low, cot)
        dk = nn(ds[plen:], q)
        if h == 0:
            dv_s[...] = dv
            dk_s[...] = dk
        else:
            dv_s[...] += dv
            dk_s[...] += dk

    pipeline([weight_stage, cot_stage, grad_stage], RATIO)
    bg_ref[0] = (dk_s[...] * SCALE).astype(BF)
    bg_ref[1] = dv_s[...].astype(BF)
    done_ref[...] = jnp.zeros_like(done_ref)


def branch_pass(at, count, earlier, q, og, vw, vg, bkv, pieces, stats):
    size, rows = q.shape[0], pieces[0].shape[1]
    plen = YH * X * rows
    operands = [q, og, vw, vg, bkv, *pieces, stats]
    return pl.pallas_call(
        functools.partial(branch_kernel, plen=plen),
        grid=(count,),
        in_specs=common_specs(size, rows, at) + [pl.BlockSpec((1, 3 * RATIO, size), lambda j: (j + at, 0, 0))]
        + [pl.BlockSpec(memory_space=pl.ANY)] * len(earlier),
        out_specs=[pl.BlockSpec((size, RATIO * HD), lambda j: (0, j + at)),
                   pl.BlockSpec((2, size, HD), lambda j: (0, 0, j + at)),
                   pl.BlockSpec((1, KVH * HD), lambda j: (0, 0))],
        out_shape=[jax.ShapeDtypeStruct(q.shape, BF), jax.ShapeDtypeStruct(bkv.shape, BF),
                   jax.ShapeDtypeStruct((1, KVH * HD), F32)],
        scratch_shapes=[
            pltpu.VMEM((plen + size, HD), BF), pltpu.VMEM((plen + size, HD), BF),
            pltpu.VMEM((size, HD), F32), pltpu.VMEM((size, HD), F32), pltpu.VMEM((size, size), F32)],
        input_output_aliases={len(operands) + i: i for i in range(min(2, len(earlier)))},
        compiler_params=pltpu.CompilerParams(vmem_limit_bytes=VMEM),
        cost_estimate=pl.CostEstimate(
            flops=count * 15 * 10**8, bytes_accessed=count * 2 * 10**6, transcendentals=count * 15 * 10**5),
    )(*operands, *earlier)


def my_place():
    return lax.axis_index("z"), lax.axis_index("yl") * CORE + lax.axis_index("c")


def wanted_at(parents_ref, my_z, pair):
    parent = parents_ref[my_z * FOUR + pair]
    behind = lax.rem(my_z - lax.div(parent, FOUR) + Z, Z)
    yl, core = lax.div(lax.rem(parent, FOUR), CORE), lax.rem(parent, CORE)
    holder = jnp.where(behind == Z // 2, core, (behind > Z // 2).astype(jnp.int32))
    ahead = jnp.where(holder == 0, behind, Z - behind)
    return yl * CORE + holder, 2 * ahead + (core != holder).astype(jnp.int32)


def ask_kernel(parents_ref, *refs):
    blocks, outs = refs[: Z // 2 + 1], refs[Z // 2 + 1 :]
    my_z, pair = my_place()
    for t, out in enumerate(outs):
        source, place = wanted_at(parents_ref, my_z, lax.rem(pair + t, FOUR))
        place = jnp.where(source == pair, place, 0)
        for k in range(Z + 1):

            @pl.when(place == k)
            def _():
                out[...] = blocks[k // 2][k % 2] if k < Z else blocks[k // 2][...]


def take_kernel(parents_ref, *refs):
    received, out = refs[:FOUR], refs[FOUR]
    my_z, pair = my_place()
    source, _ = wanted_at(parents_ref, my_z, pair)
    place = lax.rem(pair - source + FOUR, FOUR)
    for k in range(FOUR):

        @pl.when(place == k)
        def _():
            out[...] = received[k][...]


def slot_kernel(parents_ref, *refs):
    blocks, outs, acc = refs[: Z // 2 + 1], refs[Z // 2 + 2 : -1], refs[-1]
    my_z, pair = my_place()
    core = lax.rem(pair, CORE)
    for t, out in enumerate(outs):
        acc[...] = jnp.zeros_like(acc)
        for k in range(Z + 1):
            ahead, swapped = divmod(k, 2)
            from_z = lax.rem(jnp.where(core == 0, my_z - ahead + Z, my_z + ahead), Z)
            from_pair = pair - core + (1 - core if swapped else core)
            parent = parents_ref[from_z * FOUR + from_pair]
            mine = parent == my_z * FOUR + lax.rem(pair + t, FOUR)
            if ahead == 0:
                mine = jnp.logical_and(mine, core == 0)

            @pl.when(mine)
            def _():
                acc[...] += (blocks[ahead][swapped] if k < Z else blocks[ahead][...]).astype(F32)

        out[...] = acc[...].astype(out.dtype)


def choose(kernel, parents, blocks, kinds, scratch=(), after=()):
    return pl.pallas_call(
        kernel,
        in_specs=[pl.BlockSpec(memory_space=pltpu.SMEM)] + [pl.BlockSpec(memory_space=pltpu.VMEM)] * len(blocks)
        + [pl.BlockSpec(memory_space=pl.ANY)] * len(after),
        out_specs=[pl.BlockSpec(memory_space=pltpu.VMEM)] * len(kinds),
        out_shape=[jax.ShapeDtypeStruct((2, *blocks[0].shape[-2:]), kind) for kind in kinds],
        scratch_shapes=scratch,
    )(parents, *blocks, *after)


def shift(value, axis, step, size):
    return lax.ppermute(value, axis, [(i, (i + step) % size) for i in range(size)])


def spread(value, step):
    perm = [(z * CORE + c, ((z + (-step if c else step)) % Z) * CORE + c) for z in range(Z) for c in range(CORE)]
    return lax.ppermute(value, ("z", "c"), perm)


def gather_z(value):
    both = jnp.stack([value, shift(value, "c", 1, CORE)])
    far = spread(both, 2)
    near = spread(both, 1)
    return [both, near, far, spread(far, 1), spread(far[0], 2)]


def shards(queries, branch_kv, prefix_kv, out_grad, value_weight, value_grad, parents, lengths):
    asked = choose(ask_kernel, parents, gather_z(prefix_kv[0]), [BF] * FOUR)
    received = [asked[0]] + [shift(asked[t], ("yl", "c"), t, FOUR) for t in range(1, FOUR)]
    (picked,) = choose(take_kernel, parents, received, [BF])

    row = [picked] + [shift(picked, "x", k, X) for k in range(1, X)]
    pieces = row + [shift(piece, "yh", 1, YH) for piece in row]

    operands = (queries[0, 0], out_grad[0, 0], value_weight[None], value_grad[0], branch_kv[0, 0], pieces)
    values, *grads, stats = prefix_pass(lengths[0], *operands)

    back = grads[:1]
    for i in range(1, YH * X):
        jy, k = divmod(i, X)
        perm = [(b, ((b // X - jy) % YH) * X + (b % X - k) % X) for b in range(YH * X)]
        back.append(lax.ppermute(grads[i], ("yh", "x"), perm))
    *rest, done = branch_pass(0, 1, [], *operands, stats)
    share = (sum(part.astype(F32) for part in back) + done).astype(BF)

    ring = gather_z(share)
    *rest, done = branch_pass(1, 1, [*rest, share], *operands, stats)
    *rest, done = branch_pass(2, 1, [*rest, ring[2]], *operands, stats)
    acc = [pltpu.VMEM(share.shape, F32)]
    own, *others = choose(slot_kernel, parents, ring, [F32, BF, BF, BF], acc, [done])
    query_grad, branch_grad, done = branch_pass(3, 1, [*rest, own], *operands, stats)
    prefix_grad = own + done
    for t in range(1, FOUR):
        prefix_grad += shift(others[t - 1], ("yl", "c"), t, FOUR).astype(F32)
    return values[None], query_grad[None, None], branch_grad[None, None], prefix_grad[None]


def solution(mesh):
    fine = Mesh(mesh.devices.reshape(Z, YL, CORE, YH, X), ("z", "yl", "c", "yh", "x"))
    prefix, branch = ("z", "yl", "c"), ("yh", "x")
    in_specs = (
        P(prefix, branch, None, None),
        P(prefix, branch, None, None, None),
        P(prefix, None, branch, None),
        P(prefix, branch, None, None),
        P(),
        P(prefix, branch, None),
        P(),
        P(prefix, branch),
    )
    out_specs = (
        P(prefix, branch, None),
        P(prefix, branch, None, None),
        P(prefix, branch, None, None, None),
        P(prefix, None, branch, None),
    )
    return jax.shard_map(shards, mesh=fine, in_specs=in_specs, out_specs=out_specs, check_vma=False)
```

```python
import functools

import jax
import jax.numpy as jnp
from jax import lax
from jax.experimental import pallas as pl
from jax.experimental.pallas import tpu as pltpu
from jax.sharding import Mesh, PartitionSpec as P

QH = 32
KVH = 4
HD = 128
RATIO = QH // KVH
LOG2E = 1.4426950408889634
SCALE = HD**-0.5
F32 = jnp.float32
BF = jnp.bfloat16
VMEM = 56 * 1024 * 1024
Z, YL, CORE, YH, X = 8, 2, 2, 2, 4
FOUR = YL * CORE


def tn(a, b):
    return lax.dot_general(a, b, (((0,), (0,)), ((), ())), preferred_element_type=F32)


def nt(a, b):
    return lax.dot_general(a, b, (((1,), (1,)), ((), ())), preferred_element_type=F32)


def nn(a, b):
    return jnp.dot(a, b, preferred_element_type=F32)


def load_keys(k_s, v_s, pieces, bkv_ref, plen, rows):
    for i in range(YH * X):
        k_s[i * rows : (i + 1) * rows, :] = pieces[i][0]
        v_s[i * rows : (i + 1) * rows, :] = pieces[i][1]
    k_s[plen:, :] = bkv_ref[0]
    v_s[plen:, :] = bkv_ref[1]


def set_bias(bias_s):
    size = bias_s.shape[0]
    key_at = lax.broadcasted_iota(jnp.int32, (size, size), 0)
    row_at = lax.broadcasted_iota(jnp.int32, (size, size), 1)
    bias_s[...] = jnp.where(key_at <= row_at, 0.0, -1e30)


def column(row, size):
    return jnp.broadcast_to(row, (8, size)).T[:, :1]


def pipeline(stages, count):
    depth = len(stages)
    for step in range(count + depth - 1):
        for late, stage in enumerate(stages):
            if 0 <= step - late < count:
                stage(step - late)


def early_kernel(q_ref, og_ref, vw_ref, vg_ref, bkv_ref, att_ref, stat_ref, bias_s):
    size = q_ref.shape[0]

    @pl.when(pl.program_id(0) == 0)
    def _():
        set_bias(bias_s)

    val_t = bkv_ref[1].T
    state = {}

    def score_stage(h):
        s = nt(bkv_ref[0], q_ref[:, h * HD : (h + 1) * HD]) * (SCALE * LOG2E) + bias_s[...]
        top = jnp.max(s, axis=0, keepdims=True)
        p = jnp.exp2(s - top)
        stat_ref[0, h : h + 1, :] = top
        stat_ref[0, RATIO + h : RATIO + h + 1, :] = jnp.sum(p, axis=0, keepdims=True)
        state[h] = p.astype(BF)

    def value_stage(h):
        att_ref[0, h] = nn(val_t, state.pop(h))

    pipeline([score_stage, value_stage], RATIO)


def early_pass(q, og, vw, vg, bkv):
    size = q.shape[0]
    return pl.pallas_call(
        early_kernel,
        grid=(KVH,),
        in_specs=common_specs(size, 0, 0)[:5],
        out_specs=[pl.BlockSpec((1, RATIO, HD, size), lambda j: (j, 0, 0, 0)),
                   pl.BlockSpec((1, 2 * RATIO, size), lambda j: (j, 0, 0))],
        out_shape=[jax.ShapeDtypeStruct((KVH, RATIO, HD, size), F32),
                   jax.ShapeDtypeStruct((KVH, 2 * RATIO, size), F32)],
        scratch_shapes=[pltpu.VMEM((size, size), F32)],
        compiler_params=pltpu.CompilerParams(vmem_limit_bytes=VMEM),
        cost_estimate=pl.CostEstimate(flops=5 * 10**9, bytes_accessed=8 * 10**6, transcendentals=2 * 10**6),
    )(q, og, vw, vg, bkv)


def prefix_kernel(len_ref, q_ref, og_ref, vw_ref, vg_ref, bkv_ref, *rest, plen):
    pieces, att_ref, early_ref = rest[: YH * X], rest[YH * X], rest[YH * X + 1]
    val_ref, *grads, stat_ref, k_s, v_s, dk_s, dv_s, val_s = rest[YH * X + 2 :]
    j = pl.program_id(0)
    size = q_ref.shape[0]
    rows = plen // (YH * X)
    for i in range(YH * X):
        k_s[i * rows : (i + 1) * rows, :] = pieces[i][0]
        v_s[i * rows : (i + 1) * rows, :] = pieces[i][1]
    vg_col = column(vg_ref[...], size)
    live = (lax.broadcasted_iota(jnp.int32, (1, size), 1) < len_ref[0]).astype(F32)
    val_t = v_s[...].T

    @pl.when(j == 0)
    def _():
        val_s[...] = jnp.zeros_like(val_s)

    state = {}
    value_sum = [jnp.zeros((HD, size), F32)]
    vw_cols = jnp.concatenate([vw_ref[:, h * HD : (h + 1) * HD] for h in range(RATIO)], axis=0).T

    def softmax_stage(h):
        cols = slice(h * HD, (h + 1) * HD)
        q = q_ref[:, cols]
        cot = (og_ref[:, cols].astype(F32) + vg_col * vw_ref[:, cols]).astype(BF)
        s = nt(k_s[...], q) * (SCALE * LOG2E)
        early_top = early_ref[0, h : h + 1, :]
        top = jnp.maximum(jnp.max(s, axis=0, keepdims=True), early_top)
        p = jnp.exp2(s - top)
        fade = jnp.exp2(early_top - top)
        total = jnp.sum(p, axis=0, keepdims=True) + fade * early_ref[0, RATIO + h : RATIO + h + 1, :]
        part = live / total
        w = p * part
        stat_ref[0, h : h + 1, :] = top
        stat_ref[0, RATIO + h : RATIO + h + 1, :] = part
        state[h] = (q, cot, w, w.astype(BF), fade * part)

    def cot_stage(h):
        q, cot, w, low, fade = state[h]
        att = nn(val_t, low) + att_ref[0, h] * fade
        dp = nt(v_s[...], cot)
        delta = jnp.sum(cot.T.astype(F32) * att, axis=0, keepdims=True)
        stat_ref[0, 2 * RATIO + h : 2 * RATIO + h + 1, :] = delta
        value_sum[0] = value_sum[0] + att * vw_cols[:, h : h + 1]
        state[h] = (q, cot, w, low, dp, delta)

    def grad_stage(h):
        q, cot, w, low, dp, delta = state.pop(h)
        ds = (w * (dp - delta)).astype(BF)
        dv = nn(low, cot)
        dk = nn(ds, q)
        if h == 0:
            dv_s[...] = dv
            dk_s[...] = dk
        else:
            dv_s[...] += dv
            dk_s[...] += dk

    pipeline([softmax_stage, cot_stage, grad_stage], RATIO)
    val_s[...] += value_sum[0]
    dk = (dk_s[...] * SCALE).astype(BF)
    dv = dv_s[...].astype(BF)
    for i in range(YH * X):
        grads[i][0] = dk[i * rows : (i + 1) * rows]
        grads[i][1] = dv[i * rows : (i + 1) * rows]

    @pl.when(j == pl.num_programs(0) - 1)
    def _():
        val_ref[...] = jnp.sum(val_s[...], axis=0, keepdims=True)


def common_specs(size, rows, at):
    wide = RATIO * HD
    return [
        pl.BlockSpec((size, wide), lambda j: (0, j + at)),
        pl.BlockSpec((size, wide), lambda j: (0, j + at)),
        pl.BlockSpec((1, wide), lambda j: (0, j + at)),
        pl.BlockSpec((1, size), lambda j: (0, 0)),
        pl.BlockSpec((2, size, HD), lambda j: (0, 0, j + at)),
    ] + [pl.BlockSpec((2, rows, HD), lambda j: (0, 0, j + at))] * (YH * X)


def prefix_pass(lengths, q, og, vw, vg, bkv, pieces, att, early):
    size, rows = q.shape[0], pieces[0].shape[1]
    plen = YH * X * rows
    grad = jax.ShapeDtypeStruct((2, rows, KVH * HD), BF)
    grad_spec = pl.BlockSpec((2, rows, HD), lambda j: (0, 0, j))
    return pl.pallas_call(
        functools.partial(prefix_kernel, plen=plen),
        grid=(KVH,),
        in_specs=[pl.BlockSpec(memory_space=pltpu.SMEM)] + common_specs(size, rows, 0) + [
            pl.BlockSpec((1, RATIO, HD, size), lambda j: (j, 0, 0, 0)),
            pl.BlockSpec((1, 2 * RATIO, size), lambda j: (j, 0, 0))],
        out_specs=[pl.BlockSpec((1, size), lambda j: (0, 0)), *[grad_spec] * (YH * X),
                   pl.BlockSpec((1, 3 * RATIO, size), lambda j: (j, 0, 0))],
        out_shape=[jax.ShapeDtypeStruct((1, size), F32), *[grad] * (YH * X),
                   jax.ShapeDtypeStruct((KVH, 3 * RATIO, size), F32)],
        scratch_shapes=[
            pltpu.VMEM((plen, HD), BF), pltpu.VMEM((plen, HD), BF),
            pltpu.VMEM((plen, HD), F32), pltpu.VMEM((plen, HD), F32),
            pltpu.VMEM((HD, size), F32)],
        compiler_params=pltpu.CompilerParams(vmem_limit_bytes=VMEM),
        cost_estimate=pl.CostEstimate(flops=8 * 10**9, bytes_accessed=8 * 10**6, transcendentals=6 * 10**6),
    )(lengths, q, og, vw, vg, bkv, *pieces, att, early)


def branch_kernel(q_ref, og_ref, vw_ref, vg_ref, bkv_ref, *rest, plen):
    pieces, stat_ref = rest[: YH * X], rest[YH * X]
    dq_ref, bg_ref, done_ref, k_s, v_s, dk_s, dv_s, bias_s = rest[-8:]
    size = q_ref.shape[0]
    rows = plen // (YH * X)
    load_keys(k_s, v_s, pieces, bkv_ref, plen, rows)
    vg_col = column(vg_ref[...], size)
    set_bias(bias_s)
    state = {}

    def weight_stage(h):
        cols = slice(h * HD, (h + 1) * HD)
        q = q_ref[:, cols]
        cot = (og_ref[:, cols].astype(F32) + vg_col * vw_ref[:, cols]).astype(BF)
        s = nt(k_s[...], q)
        top = stat_ref[0, h : h + 1, :]
        part = stat_ref[0, RATIO + h : RATIO + h + 1, :]
        wp = jnp.exp2(s[:plen] * (SCALE * LOG2E) - top) * part
        wb = jnp.exp2(s[plen:] * (SCALE * LOG2E) + bias_s[...] - top) * part
        state[h] = (q, cot, wp, wb)

    def cot_stage(h):
        q, cot, wp, wb = state[h]
        delta = stat_ref[0, 2 * RATIO + h : 2 * RATIO + h + 1, :]
        dp = nt(v_s[...], cot)
        ds = jnp.concatenate([(wp * (dp[:plen] - delta)).astype(BF), (wb * (dp[plen:] - delta)).astype(BF)], axis=0)
        state[h] = (q, cot, wb.astype(BF), ds)

    def grad_stage(h):
        q, cot, low, ds = state.pop(h)
        dq_ref[:, h * HD : (h + 1) * HD] = (tn(ds, k_s[...]) * SCALE).astype(BF)
        dv = nn(low, cot)
        dk = nn(ds[plen:], q)
        if h == 0:
            dv_s[...] = dv
            dk_s[...] = dk
        else:
            dv_s[...] += dv
            dk_s[...] += dk

    pipeline([weight_stage, cot_stage, grad_stage], RATIO)
    bg_ref[0] = (dk_s[...] * SCALE).astype(BF)
    bg_ref[1] = dv_s[...].astype(BF)
    done_ref[...] = jnp.zeros_like(done_ref)


def branch_pass(at, count, earlier, q, og, vw, vg, bkv, pieces, stats):
    size, rows = q.shape[0], pieces[0].shape[1]
    plen = YH * X * rows
    operands = [q, og, vw, vg, bkv, *pieces, stats]
    return pl.pallas_call(
        functools.partial(branch_kernel, plen=plen),
        grid=(count,),
        in_specs=common_specs(size, rows, at) + [pl.BlockSpec((1, 3 * RATIO, size), lambda j: (j + at, 0, 0))]
        + [pl.BlockSpec(memory_space=pl.ANY)] * len(earlier),
        out_specs=[pl.BlockSpec((size, RATIO * HD), lambda j: (0, j + at)),
                   pl.BlockSpec((2, size, HD), lambda j: (0, 0, j + at)),
                   pl.BlockSpec((1, KVH * HD), lambda j: (0, 0))],
        out_shape=[jax.ShapeDtypeStruct(q.shape, BF), jax.ShapeDtypeStruct(bkv.shape, BF),
                   jax.ShapeDtypeStruct((1, KVH * HD), F32)],
        scratch_shapes=[
            pltpu.VMEM((plen + size, HD), BF), pltpu.VMEM((plen + size, HD), BF),
            pltpu.VMEM((size, HD), F32), pltpu.VMEM((size, HD), F32), pltpu.VMEM((size, size), F32)],
        input_output_aliases={len(operands) + i: i for i in range(min(2, len(earlier)))},
        compiler_params=pltpu.CompilerParams(vmem_limit_bytes=VMEM),
        cost_estimate=pl.CostEstimate(
            flops=count * 15 * 10**8, bytes_accessed=count * 2 * 10**6, transcendentals=count * 15 * 10**5),
    )(*operands, *earlier)


def my_place():
    return lax.axis_index("z"), lax.axis_index("yl") * CORE + lax.axis_index("c")


def wanted_at(parents_ref, my_z, pair):
    parent = parents_ref[my_z * FOUR + pair]
    behind = lax.rem(my_z - lax.div(parent, FOUR) + Z, Z)
    yl, core = lax.div(lax.rem(parent, FOUR), CORE), lax.rem(parent, CORE)
    holder = jnp.where(behind == Z // 2, core, (behind > Z // 2).astype(jnp.int32))
    ahead = jnp.where(holder == 0, behind, Z - behind)
    return yl * CORE + holder, 2 * ahead + (core != holder).astype(jnp.int32)


def ask_kernel(parents_ref, *refs):
    blocks, outs = refs[: Z // 2 + 1], refs[Z // 2 + 2 :]
    my_z, pair = my_place()
    for t, out in enumerate(outs):
        source, place = wanted_at(parents_ref, my_z, lax.rem(pair + t, FOUR))
        place = jnp.where(source == pair, place, 0)
        for k in range(Z + 1):

            @pl.when(place == k)
            def _():
                out[...] = blocks[k // 2][k % 2] if k < Z else blocks[k // 2][...]


def take_kernel(parents_ref, *refs):
    received, out = refs[:FOUR], refs[FOUR]
    my_z, pair = my_place()
    source, _ = wanted_at(parents_ref, my_z, pair)
    place = lax.rem(pair - source + FOUR, FOUR)
    for k in range(FOUR):

        @pl.when(place == k)
        def _():
            out[...] = received[k][...]


def slot_kernel(parents_ref, *refs):
    blocks, outs, acc = refs[: Z // 2 + 1], refs[Z // 2 + 2 : -1], refs[-1]
    my_z, pair = my_place()
    core = lax.rem(pair, CORE)
    for t, out in enumerate(outs):
        acc[...] = jnp.zeros_like(acc)
        for k in range(Z + 1):
            ahead, swapped = divmod(k, 2)
            from_z = lax.rem(jnp.where(core == 0, my_z - ahead + Z, my_z + ahead), Z)
            from_pair = pair - core + (1 - core if swapped else core)
            parent = parents_ref[from_z * FOUR + from_pair]
            mine = parent == my_z * FOUR + lax.rem(pair + t, FOUR)
            if ahead == 0:
                mine = jnp.logical_and(mine, core == 0)

            @pl.when(mine)
            def _():
                acc[...] += (blocks[ahead][swapped] if k < Z else blocks[ahead][...]).astype(F32)

        out[...] = acc[...].astype(out.dtype)


def choose(kernel, parents, blocks, kinds, scratch=(), after=()):
    return pl.pallas_call(
        kernel,
        in_specs=[pl.BlockSpec(memory_space=pltpu.SMEM)] + [pl.BlockSpec(memory_space=pltpu.VMEM)] * len(blocks)
        + [pl.BlockSpec(memory_space=pl.ANY)] * len(after),
        out_specs=[pl.BlockSpec(memory_space=pltpu.VMEM)] * len(kinds),
        out_shape=[jax.ShapeDtypeStruct((2, *blocks[0].shape[-2:]), kind) for kind in kinds],
        scratch_shapes=scratch,
    )(parents, *blocks, *after)


def shift(value, axis, step, size):
    return lax.ppermute(value, axis, [(i, (i + step) % size) for i in range(size)])


def spread(value, step):
    perm = [(z * CORE + c, ((z + (-step if c else step)) % Z) * CORE + c) for z in range(Z) for c in range(CORE)]
    return lax.ppermute(value, ("z", "c"), perm)


def gather_z(value):
    both = jnp.stack([value, shift(value, "c", 1, CORE)])
    far = spread(both, 2)
    near = spread(both, 1)
    return [both, near, far, spread(far, 1), spread(far[0], 2)]


def shards(queries, branch_kv, prefix_kv, out_grad, value_weight, value_grad, parents, lengths):
    own_args = (queries[0, 0], out_grad[0, 0], value_weight[None], value_grad[0], branch_kv[0, 0])
    att, early = early_pass(*own_args)
    asked = choose(ask_kernel, parents, gather_z(prefix_kv[0]), [BF] * FOUR, after=[early])
    received = [asked[0]] + [shift(asked[t], ("yl", "c"), t, FOUR) for t in range(1, FOUR)]
    (picked,) = choose(take_kernel, parents, received, [BF])

    row = [picked] + [shift(picked, "x", k, X) for k in range(1, X)]
    pieces = row + [shift(piece, "yh", 1, YH) for piece in row]

    operands = (*own_args, pieces)
    values, *grads, stats = prefix_pass(lengths[0], *operands, att, early)

    back = grads[:1]
    for i in range(1, YH * X):
        jy, k = divmod(i, X)
        perm = [(b, ((b // X - jy) % YH) * X + (b % X - k) % X) for b in range(YH * X)]
        back.append(lax.ppermute(grads[i], ("yh", "x"), perm))
    *rest, done = branch_pass(0, 1, [], *operands, stats)
    share = (sum(part.astype(F32) for part in back) + done).astype(BF)

    ring = gather_z(share)
    *rest, done = branch_pass(1, 1, [*rest, share], *operands, stats)
    *rest, done = branch_pass(2, 1, [*rest, ring[2]], *operands, stats)
    acc = [pltpu.VMEM(share.shape, F32)]
    own, *others = choose(slot_kernel, parents, ring, [F32, BF, BF, BF], acc, [done])
    query_grad, branch_grad, done = branch_pass(3, 1, [*rest, own], *operands, stats)
    prefix_grad = own + done
    for t in range(1, FOUR):
        prefix_grad += shift(others[t - 1], ("yl", "c"), t, FOUR).astype(F32)
    return values[None], query_grad[None, None], branch_grad[None, None], prefix_grad[None]


def solution(mesh):
    fine = Mesh(mesh.devices.reshape(Z, YL, CORE, YH, X), ("z", "yl", "c", "yh", "x"))
    prefix, branch = ("z", "yl", "c"), ("yh", "x")
    in_specs = (
        P(prefix, branch, None, None),
        P(prefix, branch, None, None, None),
        P(prefix, None, branch, None),
        P(prefix, branch, None, None),
        P(),
        P(prefix, branch, None),
        P(),
        P(prefix, branch),
    )
    out_specs = (
        P(prefix, branch, None),
        P(prefix, branch, None, None),
        P(prefix, branch, None, None, None),
        P(prefix, None, branch, None),
    )
    return jax.shard_map(shards, mesh=fine, in_specs=in_specs, out_specs=out_specs, check_vma=False)
```

```python
import functools

import jax
import jax.numpy as jnp
from jax import lax
from jax.experimental import pallas as pl
from jax.experimental.pallas import tpu as pltpu
from jax.sharding import Mesh, PartitionSpec as P

QH = 32
KVH = 4
HD = 128
RATIO = QH // KVH
LOG2E = 1.4426950408889634
SCALE = HD**-0.5
F32 = jnp.float32
BF = jnp.bfloat16
VMEM = 56 * 1024 * 1024
Z, YL, CORE, YH, X = 8, 2, 2, 2, 4
FOUR = YL * CORE


def tn(a, b):
    return lax.dot_general(a, b, (((0,), (0,)), ((), ())), preferred_element_type=F32)


def nt(a, b):
    return lax.dot_general(a, b, (((1,), (1,)), ((), ())), preferred_element_type=F32)


def nn(a, b):
    return jnp.dot(a, b, preferred_element_type=F32)


def load_keys(k_s, v_s, pieces, bkv_ref, plen, rows):
    for i in range(YH * X):
        k_s[i * rows : (i + 1) * rows, :] = pieces[i][0]
        v_s[i * rows : (i + 1) * rows, :] = pieces[i][1]
    k_s[plen:, :] = bkv_ref[0]
    v_s[plen:, :] = bkv_ref[1]


def set_bias(bias_s):
    size = bias_s.shape[0]
    key_at = lax.broadcasted_iota(jnp.int32, (size, size), 0)
    row_at = lax.broadcasted_iota(jnp.int32, (size, size), 1)
    bias_s[...] = jnp.where(key_at <= row_at, 0.0, -1e30)


def column(row, size):
    return jnp.broadcast_to(row, (8, size)).T[:, :1]


def pipeline(stages, count):
    depth = len(stages)
    for step in range(count + depth - 1):
        for late, stage in enumerate(stages):
            if 0 <= step - late < count:
                stage(step - late)


def early_kernel(q_ref, og_ref, vw_ref, vg_ref, bkv_ref, att_ref, stat_ref, bias_s):
    size = q_ref.shape[0]

    @pl.when(pl.program_id(0) == 0)
    def _():
        set_bias(bias_s)

    val_t = bkv_ref[1].T
    state = {}

    def score_stage(h):
        s = nt(bkv_ref[0], q_ref[:, h * HD : (h + 1) * HD]) * (SCALE * LOG2E) + bias_s[...]
        top = jnp.max(s, axis=0, keepdims=True)
        p = jnp.exp2(s - top)
        stat_ref[0, h : h + 1, :] = top
        stat_ref[0, RATIO + h : RATIO + h + 1, :] = jnp.sum(p, axis=0, keepdims=True)
        state[h] = p.astype(BF)

    def value_stage(h):
        att_ref[0, h] = nn(val_t, state.pop(h))

    pipeline([score_stage, value_stage], RATIO)


def early_pass(q, og, vw, vg, bkv):
    size = q.shape[0]
    return pl.pallas_call(
        early_kernel,
        grid=(KVH,),
        in_specs=common_specs(size, 0, 0)[:5],
        out_specs=[pl.BlockSpec((1, RATIO, HD, size), lambda j: (j, 0, 0, 0)),
                   pl.BlockSpec((1, 2 * RATIO, size), lambda j: (j, 0, 0))],
        out_shape=[jax.ShapeDtypeStruct((KVH, RATIO, HD, size), F32),
                   jax.ShapeDtypeStruct((KVH, 2 * RATIO, size), F32)],
        scratch_shapes=[pltpu.VMEM((size, size), F32)],
        compiler_params=pltpu.CompilerParams(vmem_limit_bytes=VMEM),
        cost_estimate=pl.CostEstimate(flops=5 * 10**9, bytes_accessed=8 * 10**6, transcendentals=2 * 10**6),
    )(q, og, vw, vg, bkv)


def prefix_kernel(len_ref, q_ref, og_ref, vw_ref, vg_ref, bkv_ref, *rest, plen):
    pieces, att_ref, early_ref = rest[: YH * X], rest[YH * X], rest[YH * X + 1]
    val_ref, *grads, stat_ref, k_s, v_s, dk_s, dv_s, val_s = rest[YH * X + 2 :]
    j = pl.program_id(0)
    size = q_ref.shape[0]
    rows = plen // (YH * X)
    for i in range(YH * X):
        k_s[i * rows : (i + 1) * rows, :] = pieces[i][0]
        v_s[i * rows : (i + 1) * rows, :] = pieces[i][1]
    vg_col = column(vg_ref[...], size)
    live = (lax.broadcasted_iota(jnp.int32, (1, size), 1) < len_ref[0]).astype(F32)
    val_t = v_s[...].T

    @pl.when(j == 0)
    def _():
        val_s[...] = jnp.zeros_like(val_s)

    state = {}
    value_sum = [jnp.zeros((HD, size), F32)]
    vw_cols = jnp.concatenate([vw_ref[:, h * HD : (h + 1) * HD] for h in range(RATIO)], axis=0).T

    def softmax_stage(h):
        cols = slice(h * HD, (h + 1) * HD)
        q = q_ref[:, cols]
        cot = (og_ref[:, cols].astype(F32) + vg_col * vw_ref[:, cols]).astype(BF)
        s = nt(k_s[...], q) * (SCALE * LOG2E)
        early_top = early_ref[0, h : h + 1, :]
        top = jnp.maximum(jnp.max(s, axis=0, keepdims=True), early_top)
        p = jnp.exp2(s - top)
        fade = jnp.exp2(early_top - top)
        total = jnp.sum(p, axis=0, keepdims=True) + fade * early_ref[0, RATIO + h : RATIO + h + 1, :]
        part = live / total
        w = p * part
        stat_ref[0, h : h + 1, :] = top
        stat_ref[0, RATIO + h : RATIO + h + 1, :] = part
        state[h] = (q, cot, w, w.astype(BF), fade * part)

    def cot_stage(h):
        q, cot, w, low, fade = state[h]
        att = nn(val_t, low) + att_ref[0, h] * fade
        dp = nt(v_s[...], cot)
        delta = jnp.sum(cot.T.astype(F32) * att, axis=0, keepdims=True)
        stat_ref[0, 2 * RATIO + h : 2 * RATIO + h + 1, :] = delta
        value_sum[0] = value_sum[0] + att * vw_cols[:, h : h + 1]
        state[h] = (q, cot, w, low, dp, delta)

    def grad_stage(h):
        q, cot, w, low, dp, delta = state.pop(h)
        ds = (w * (dp - delta)).astype(BF)
        dv = nn(low, cot)
        dk = nn(ds, q)
        if h == 0:
            dv_s[...] = dv
            dk_s[...] = dk
        else:
            dv_s[...] += dv
            dk_s[...] += dk

    pipeline([softmax_stage, cot_stage, grad_stage], RATIO)
    val_s[...] += value_sum[0]
    dk = (dk_s[...] * SCALE).astype(BF)
    dv = dv_s[...].astype(BF)
    for i in range(YH * X):
        grads[i][0] = dk[i * rows : (i + 1) * rows]
        grads[i][1] = dv[i * rows : (i + 1) * rows]

    @pl.when(j == pl.num_programs(0) - 1)
    def _():
        val_ref[...] = jnp.sum(val_s[...], axis=0, keepdims=True)


def common_specs(size, rows, at):
    wide = RATIO * HD
    return [
        pl.BlockSpec((size, wide), lambda j: (0, j + at)),
        pl.BlockSpec((size, wide), lambda j: (0, j + at)),
        pl.BlockSpec((1, wide), lambda j: (0, j + at)),
        pl.BlockSpec((1, size), lambda j: (0, 0)),
        pl.BlockSpec((2, size, HD), lambda j: (0, 0, j + at)),
    ] + [pl.BlockSpec((2, rows, HD), lambda j: (0, 0, j + at))] * (YH * X)


def prefix_pass(lengths, q, og, vw, vg, bkv, pieces, att, early):
    size, rows = q.shape[0], pieces[0].shape[1]
    plen = YH * X * rows
    grad = jax.ShapeDtypeStruct((2, rows, KVH * HD), BF)
    grad_spec = pl.BlockSpec((2, rows, HD), lambda j: (0, 0, j))
    return pl.pallas_call(
        functools.partial(prefix_kernel, plen=plen),
        grid=(KVH,),
        in_specs=[pl.BlockSpec(memory_space=pltpu.SMEM)] + common_specs(size, rows, 0) + [
            pl.BlockSpec((1, RATIO, HD, size), lambda j: (j, 0, 0, 0)),
            pl.BlockSpec((1, 2 * RATIO, size), lambda j: (j, 0, 0))],
        out_specs=[pl.BlockSpec((1, size), lambda j: (0, 0)), *[grad_spec] * (YH * X),
                   pl.BlockSpec((1, 3 * RATIO, size), lambda j: (j, 0, 0))],
        out_shape=[jax.ShapeDtypeStruct((1, size), F32), *[grad] * (YH * X),
                   jax.ShapeDtypeStruct((KVH, 3 * RATIO, size), F32)],
        scratch_shapes=[
            pltpu.VMEM((plen, HD), BF), pltpu.VMEM((plen, HD), BF),
            pltpu.VMEM((plen, HD), F32), pltpu.VMEM((plen, HD), F32),
            pltpu.VMEM((HD, size), F32)],
        compiler_params=pltpu.CompilerParams(vmem_limit_bytes=VMEM),
        cost_estimate=pl.CostEstimate(flops=8 * 10**9, bytes_accessed=8 * 10**6, transcendentals=6 * 10**6),
    )(lengths, q, og, vw, vg, bkv, *pieces, att, early)


def branch_kernel(q_ref, og_ref, vw_ref, vg_ref, bkv_ref, *rest, plen):
    pieces, stat_ref = rest[: YH * X], rest[YH * X]
    dq_ref, bg_ref, done_ref, k_s, v_s, dk_s, dv_s, bias_s = rest[-8:]
    size = q_ref.shape[0]
    rows = plen // (YH * X)
    load_keys(k_s, v_s, pieces, bkv_ref, plen, rows)
    vg_col = column(vg_ref[...], size)
    set_bias(bias_s)
    state = {}

    def weight_stage(h):
        cols = slice(h * HD, (h + 1) * HD)
        q = q_ref[:, cols]
        cot = (og_ref[:, cols].astype(F32) + vg_col * vw_ref[:, cols]).astype(BF)
        s = nt(k_s[...], q)
        top = stat_ref[0, h : h + 1, :]
        part = stat_ref[0, RATIO + h : RATIO + h + 1, :]
        wp = jnp.exp2(s[:plen] * (SCALE * LOG2E) - top) * part
        wb = jnp.exp2(s[plen:] * (SCALE * LOG2E) + bias_s[...] - top) * part
        state[h] = (q, cot, wp, wb)

    def cot_stage(h):
        q, cot, wp, wb = state[h]
        delta = stat_ref[0, 2 * RATIO + h : 2 * RATIO + h + 1, :]
        dp = nt(v_s[...], cot)
        ds = jnp.concatenate([(wp * (dp[:plen] - delta)).astype(BF), (wb * (dp[plen:] - delta)).astype(BF)], axis=0)
        state[h] = (q, cot, wb.astype(BF), ds)

    def grad_stage(h):
        q, cot, low, ds = state.pop(h)
        dq_ref[:, h * HD : (h + 1) * HD] = (tn(ds, k_s[...]) * SCALE).astype(BF)
        dv = nn(low, cot)
        dk = nn(ds[plen:], q)
        if h == 0:
            dv_s[...] = dv
            dk_s[...] = dk
        else:
            dv_s[...] += dv
            dk_s[...] += dk

    pipeline([weight_stage, cot_stage, grad_stage], RATIO)
    bg_ref[0] = (dk_s[...] * SCALE).astype(BF)
    bg_ref[1] = dv_s[...].astype(BF)
    done_ref[...] = jnp.zeros_like(done_ref)


def branch_pass(at, count, earlier, q, og, vw, vg, bkv, pieces, stats):
    size, rows = q.shape[0], pieces[0].shape[1]
    plen = YH * X * rows
    operands = [q, og, vw, vg, bkv, *pieces, stats]
    return pl.pallas_call(
        functools.partial(branch_kernel, plen=plen),
        grid=(count,),
        in_specs=common_specs(size, rows, at) + [pl.BlockSpec((1, 3 * RATIO, size), lambda j: (j + at, 0, 0))]
        + [pl.BlockSpec(memory_space=pl.ANY)] * len(earlier),
        out_specs=[pl.BlockSpec((size, RATIO * HD), lambda j: (0, j + at)),
                   pl.BlockSpec((2, size, HD), lambda j: (0, 0, j + at)),
                   pl.BlockSpec((1, KVH * HD), lambda j: (0, 0))],
        out_shape=[jax.ShapeDtypeStruct(q.shape, BF), jax.ShapeDtypeStruct(bkv.shape, BF),
                   jax.ShapeDtypeStruct((1, KVH * HD), F32)],
        scratch_shapes=[
            pltpu.VMEM((plen + size, HD), BF), pltpu.VMEM((plen + size, HD), BF),
            pltpu.VMEM((size, HD), F32), pltpu.VMEM((size, HD), F32), pltpu.VMEM((size, size), F32)],
        input_output_aliases={len(operands) + i: i for i in range(min(2, len(earlier)))},
        compiler_params=pltpu.CompilerParams(vmem_limit_bytes=VMEM),
        cost_estimate=pl.CostEstimate(
            flops=count * 15 * 10**8, bytes_accessed=count * 2 * 10**6, transcendentals=count * 15 * 10**5),
    )(*operands, *earlier)


def my_place():
    return lax.axis_index("z"), lax.axis_index("yl") * CORE + lax.axis_index("c")


def ask_kernel(parents_ref, *refs):
    ring, outs = refs[:Z], refs[Z + 1 :]
    my_z, pair = my_place()
    for t, out in enumerate(outs):
        parent = parents_ref[my_z * FOUR + ((pair + t) & (FOUR - 1))]
        place = (my_z - (parent >> 2)) & (Z - 1)
        for k in range(Z):

            @pl.when(place == k)
            def _():
                out[...] = ring[k][...]


def take_kernel(parents_ref, *refs):
    received, out = refs[:FOUR], refs[FOUR]
    my_z, pair = my_place()
    place = (pair - parents_ref[my_z * FOUR + pair]) & (FOUR - 1)
    for k in range(FOUR):

        @pl.when(place == k)
        def _():
            out[...] = received[k][...]


def slot_kernel(parents_ref, *refs):
    ring, outs, acc = refs[:Z], refs[Z + 1 : -1], refs[-1]
    my_z, pair = my_place()
    for t, out in enumerate(outs):
        acc[...] = jnp.zeros_like(acc)
        for k in range(Z):
            parent = parents_ref[((my_z - k) & (Z - 1)) * FOUR + pair]

            @pl.when(parent == my_z * FOUR + ((pair + t) & (FOUR - 1)))
            def _():
                acc[...] += ring[k][...].astype(F32)

        out[...] = acc[...].astype(out.dtype)


def choose(kernel, parents, blocks, kinds, scratch=(), after=()):
    return pl.pallas_call(
        kernel,
        in_specs=[pl.BlockSpec(memory_space=pltpu.SMEM)] + [pl.BlockSpec(memory_space=pltpu.VMEM)] * len(blocks)
        + [pl.BlockSpec(memory_space=pl.ANY)] * len(after),
        out_specs=[pl.BlockSpec(memory_space=pltpu.VMEM)] * len(kinds),
        out_shape=[jax.ShapeDtypeStruct((2, *blocks[0].shape[-2:]), kind) for kind in kinds],
        scratch_shapes=scratch,
    )(parents, *blocks, *after)


def shift(value, axis, step, size):
    return lax.ppermute(value, axis, [(i, (i + step) % size) for i in range(size)])


def gather_z(value):
    got = {0: value}
    for k in (2, Z - 2, 1, Z - 1):
        got[k] = shift(value, "z", k, Z)
    got[4] = shift(got[2], "z", 2, Z)
    got[3] = shift(got[2], "z", 1, Z)
    got[5] = shift(got[6], "z", -1, Z)
    return [got[k] for k in range(Z)]


def shards(queries, branch_kv, prefix_kv, out_grad, value_weight, value_grad, parents, lengths):
    own_args = (queries[0, 0], out_grad[0, 0], value_weight[None], value_grad[0], branch_kv[0, 0])
    att, early = early_pass(*own_args)
    asked = choose(ask_kernel, parents, gather_z(prefix_kv[0]), [BF] * FOUR, after=[early])
    received = [asked[0]] + [shift(asked[t], ("yl", "c"), t, FOUR) for t in range(1, FOUR)]
    (picked,) = choose(take_kernel, parents, received, [BF])

    row = [picked] + [shift(picked, "x", k, X) for k in range(1, X)]
    pieces = row + [shift(piece, "yh", 1, YH) for piece in row]

    operands = (*own_args, pieces)
    values, *grads, stats = prefix_pass(lengths[0], *operands, att, early)

    back = grads[:1]
    for i in range(1, YH * X):
        jy, k = divmod(i, X)
        perm = [(b, ((b // X - jy) % YH) * X + (b % X - k) % X) for b in range(YH * X)]
        back.append(lax.ppermute(grads[i], ("yh", "x"), perm))
    *rest, done = branch_pass(0, 1, [], *operands, stats)
    share = (sum(part.astype(F32) for part in back) + done).astype(BF)

    ring = gather_z(share)
    *rest, done = branch_pass(1, 1, [*rest, share], *operands, stats)
    *rest, done = branch_pass(2, 1, [*rest, ring[2]], *operands, stats)
    acc = [pltpu.VMEM(share.shape, F32)]
    own, *others = choose(slot_kernel, parents, ring, [F32, BF, BF, BF], acc, [done])
    query_grad, branch_grad, done = branch_pass(3, 1, [*rest, own], *operands, stats)
    prefix_grad = own + done
    for t in range(1, FOUR):
        prefix_grad += shift(others[t - 1], ("yl", "c"), t, FOUR).astype(F32)
    return values[None], query_grad[None, None], branch_grad[None, None], prefix_grad[None]


def solution(mesh):
    fine = Mesh(mesh.devices.reshape(Z, YL, CORE, YH, X), ("z", "yl", "c", "yh", "x"))
    prefix, branch = ("z", "yl", "c"), ("yh", "x")
    in_specs = (
        P(prefix, branch, None, None),
        P(prefix, branch, None, None, None),
        P(prefix, None, branch, None),
        P(prefix, branch, None, None),
        P(),
        P(prefix, branch, None),
        P(),
        P(prefix, branch),
    )
    out_specs = (
        P(prefix, branch, None),
        P(prefix, branch, None, None),
        P(prefix, branch, None, None, None),
        P(prefix, None, branch, None),
    )
    return jax.shard_map(shards, mesh=fine, in_specs=in_specs, out_specs=out_specs, check_vma=False)
```

```python
import functools

import jax
import jax.numpy as jnp
from jax import lax
from jax.experimental import pallas as pl
from jax.experimental.pallas import tpu as pltpu
from jax.sharding import Mesh, PartitionSpec as P

QH = 32
KVH = 4
HD = 128
RATIO = QH // KVH
LOG2E = 1.4426950408889634
SCALE = HD**-0.5
F32 = jnp.float32
BF = jnp.bfloat16
VMEM = 56 * 1024 * 1024
Z, YL, CORE, YH, X = 8, 2, 2, 2, 4
FOUR = YL * CORE


def tn(a, b):
    return lax.dot_general(a, b, (((0,), (0,)), ((), ())), preferred_element_type=F32)


def nt(a, b):
    return lax.dot_general(a, b, (((1,), (1,)), ((), ())), preferred_element_type=F32)


def nn(a, b):
    return jnp.dot(a, b, preferred_element_type=F32)


def load_keys(k_s, v_s, pieces, bkv_ref, plen, rows):
    for i in range(YH * X):
        k_s[i * rows : (i + 1) * rows, :] = pieces[i][0]
        v_s[i * rows : (i + 1) * rows, :] = pieces[i][1]
    k_s[plen:, :] = bkv_ref[0]
    v_s[plen:, :] = bkv_ref[1]


def set_bias(bias_s):
    size = bias_s.shape[0]
    key_at = lax.broadcasted_iota(jnp.int32, (size, size), 0)
    row_at = lax.broadcasted_iota(jnp.int32, (size, size), 1)
    bias_s[...] = jnp.where(key_at <= row_at, 0.0, -1e30)


def column(row, size):
    return jnp.broadcast_to(row, (8, size)).T[:, :1]


def pipeline(stages, count):
    depth = len(stages)
    for step in range(count + depth - 1):
        for late, stage in enumerate(stages):
            if 0 <= step - late < count:
                stage(step - late)


def early_kernel(q_ref, og_ref, vw_ref, vg_ref, bkv_ref, att_ref, stat_ref, bias_s):
    size = q_ref.shape[0]

    @pl.when(pl.program_id(0) == 0)
    def _():
        set_bias(bias_s)

    val_t = bkv_ref[1].T
    state = {}

    def score_stage(h):
        s = nt(bkv_ref[0], q_ref[:, h * HD : (h + 1) * HD]) * (SCALE * LOG2E) + bias_s[...]
        top = jnp.max(s, axis=0, keepdims=True)
        p = jnp.exp2(s - top)
        stat_ref[0, h : h + 1, :] = top
        stat_ref[0, RATIO + h : RATIO + h + 1, :] = jnp.sum(p, axis=0, keepdims=True)
        state[h] = p.astype(BF)

    def value_stage(h):
        att_ref[0, h] = nn(val_t, state.pop(h))

    pipeline([score_stage, value_stage], RATIO)


def early_pass(q, og, vw, vg, bkv):
    size = q.shape[0]
    return pl.pallas_call(
        early_kernel,
        grid=(KVH,),
        in_specs=common_specs(size, 0, 0)[:5],
        out_specs=[pl.BlockSpec((1, RATIO, HD, size), lambda j: (j, 0, 0, 0)),
                   pl.BlockSpec((1, 2 * RATIO, size), lambda j: (j, 0, 0))],
        out_shape=[jax.ShapeDtypeStruct((KVH, RATIO, HD, size), F32),
                   jax.ShapeDtypeStruct((KVH, 2 * RATIO, size), F32)],
        scratch_shapes=[pltpu.VMEM((size, size), F32)],
        compiler_params=pltpu.CompilerParams(vmem_limit_bytes=VMEM),
        cost_estimate=pl.CostEstimate(flops=5 * 10**9, bytes_accessed=8 * 10**6, transcendentals=2 * 10**6),
    )(q, og, vw, vg, bkv)


def prefix_kernel(len_ref, q_ref, og_ref, vw_ref, vg_ref, bkv_ref, *rest, plen):
    pieces, att_ref, early_ref = rest[: YH * X], rest[YH * X], rest[YH * X + 1]
    val_ref, *grads, stat_ref, k_s, v_s, dk_s, dv_s, val_s = rest[YH * X + 2 :]
    j = pl.program_id(0)
    size = q_ref.shape[0]
    rows = plen // (YH * X)
    for i in range(YH * X):
        k_s[i * rows : (i + 1) * rows, :] = pieces[i][0]
        v_s[i * rows : (i + 1) * rows, :] = pieces[i][1]
    vg_col = column(vg_ref[...], size)
    live = (lax.broadcasted_iota(jnp.int32, (1, size), 1) < len_ref[0]).astype(F32)
    val_t = v_s[...].T

    @pl.when(j == 0)
    def _():
        val_s[...] = jnp.zeros_like(val_s)

    state = {}
    value_sum = [jnp.zeros((HD, size), F32)]
    vw_cols = jnp.concatenate([vw_ref[:, h * HD : (h + 1) * HD] for h in range(RATIO)], axis=0).T

    def softmax_stage(h):
        cols = slice(h * HD, (h + 1) * HD)
        q = q_ref[:, cols]
        cot = (og_ref[:, cols].astype(F32) + vg_col * vw_ref[:, cols]).astype(BF)
        s = nt(k_s[...], q) * (SCALE * LOG2E)
        early_top = early_ref[0, h : h + 1, :]
        top = jnp.maximum(jnp.max(s, axis=0, keepdims=True), early_top)
        p = jnp.exp2(s - top)
        fade = jnp.exp2(early_top - top)
        total = jnp.sum(p, axis=0, keepdims=True) + fade * early_ref[0, RATIO + h : RATIO + h + 1, :]
        part = live / total
        w = p * part
        stat_ref[0, h : h + 1, :] = top
        stat_ref[0, RATIO + h : RATIO + h + 1, :] = part
        state[h] = (q, cot, w, w.astype(BF), fade * part)

    def cot_stage(h):
        q, cot, w, low, fade = state[h]
        att = nn(val_t, low) + att_ref[0, h] * fade
        dp = nt(v_s[...], cot)
        delta = jnp.sum(cot.T.astype(F32) * att, axis=0, keepdims=True)
        stat_ref[0, 2 * RATIO + h : 2 * RATIO + h + 1, :] = delta
        value_sum[0] = value_sum[0] + att * vw_cols[:, h : h + 1]
        state[h] = (q, cot, w, low, dp, delta)

    def grad_stage(h):
        q, cot, w, low, dp, delta = state.pop(h)
        ds = (w * (dp - delta)).astype(BF)
        dv = nn(low, cot)
        dk = nn(ds, q)
        if h == 0:
            dv_s[...] = dv
            dk_s[...] = dk
        else:
            dv_s[...] += dv
            dk_s[...] += dk

    pipeline([softmax_stage, cot_stage, grad_stage], RATIO)
    val_s[...] += value_sum[0]
    dk = (dk_s[...] * SCALE).astype(BF)
    dv = dv_s[...].astype(BF)
    for i in range(YH * X):
        grads[i][0] = dk[i * rows : (i + 1) * rows]
        grads[i][1] = dv[i * rows : (i + 1) * rows]

    @pl.when(j == pl.num_programs(0) - 1)
    def _():
        val_ref[...] = jnp.sum(val_s[...], axis=0, keepdims=True)


def common_specs(size, rows, at):
    wide = RATIO * HD
    return [
        pl.BlockSpec((size, wide), lambda j: (0, j + at)),
        pl.BlockSpec((size, wide), lambda j: (0, j + at)),
        pl.BlockSpec((1, wide), lambda j: (0, j + at)),
        pl.BlockSpec((1, size), lambda j: (0, 0)),
        pl.BlockSpec((2, size, HD), lambda j: (0, 0, j + at)),
    ] + [pl.BlockSpec((2, rows, HD), lambda j: (0, 0, j + at))] * (YH * X)


def prefix_pass(lengths, q, og, vw, vg, bkv, pieces, att, early):
    size, rows = q.shape[0], pieces[0].shape[1]
    plen = YH * X * rows
    grad = jax.ShapeDtypeStruct((2, rows, KVH * HD), BF)
    grad_spec = pl.BlockSpec((2, rows, HD), lambda j: (0, 0, j))
    return pl.pallas_call(
        functools.partial(prefix_kernel, plen=plen),
        grid=(KVH,),
        in_specs=[pl.BlockSpec(memory_space=pltpu.SMEM)] + common_specs(size, rows, 0) + [
            pl.BlockSpec((1, RATIO, HD, size), lambda j: (j, 0, 0, 0)),
            pl.BlockSpec((1, 2 * RATIO, size), lambda j: (j, 0, 0))],
        out_specs=[pl.BlockSpec((1, size), lambda j: (0, 0)), *[grad_spec] * (YH * X),
                   pl.BlockSpec((1, 3 * RATIO, size), lambda j: (j, 0, 0))],
        out_shape=[jax.ShapeDtypeStruct((1, size), F32), *[grad] * (YH * X),
                   jax.ShapeDtypeStruct((KVH, 3 * RATIO, size), F32)],
        scratch_shapes=[
            pltpu.VMEM((plen, HD), BF), pltpu.VMEM((plen, HD), BF),
            pltpu.VMEM((plen, HD), F32), pltpu.VMEM((plen, HD), F32),
            pltpu.VMEM((HD, size), F32)],
        compiler_params=pltpu.CompilerParams(vmem_limit_bytes=VMEM),
        cost_estimate=pl.CostEstimate(flops=8 * 10**9, bytes_accessed=8 * 10**6, transcendentals=6 * 10**6),
    )(lengths, q, og, vw, vg, bkv, *pieces, att, early)


def branch_kernel(q_ref, og_ref, vw_ref, vg_ref, bkv_ref, *rest, plen):
    pieces, stat_ref = rest[: YH * X], rest[YH * X]
    dq_ref, bg_ref, done_ref, k_s, v_s, dk_s, dv_s, bias_s = rest[-8:]
    size = q_ref.shape[0]
    rows = plen // (YH * X)
    load_keys(k_s, v_s, pieces, bkv_ref, plen, rows)
    vg_col = column(vg_ref[...], size)
    set_bias(bias_s)
    state = {}

    def weight_stage(h):
        cols = slice(h * HD, (h + 1) * HD)
        q = q_ref[:, cols]
        cot = (og_ref[:, cols].astype(F32) + vg_col * vw_ref[:, cols]).astype(BF)
        s = nt(k_s[...], q)
        top = stat_ref[0, h : h + 1, :]
        part = stat_ref[0, RATIO + h : RATIO + h + 1, :]
        wp = jnp.exp2(s[:plen] * (SCALE * LOG2E) - top) * part
        wb = jnp.exp2(s[plen:] * (SCALE * LOG2E) + bias_s[...] - top) * part
        state[h] = (q, cot, wp, wb)

    def cot_stage(h):
        q, cot, wp, wb = state[h]
        delta = stat_ref[0, 2 * RATIO + h : 2 * RATIO + h + 1, :]
        dp = nt(v_s[...], cot)
        ds = jnp.concatenate([(wp * (dp[:plen] - delta)).astype(BF), (wb * (dp[plen:] - delta)).astype(BF)], axis=0)
        state[h] = (q, cot, wb.astype(BF), ds)

    def grad_stage(h):
        q, cot, low, ds = state.pop(h)
        dq_ref[:, h * HD : (h + 1) * HD] = (tn(ds, k_s[...]) * SCALE).astype(BF)
        dv = nn(low, cot)
        dk = nn(ds[plen:], q)
        if h == 0:
            dv_s[...] = dv
            dk_s[...] = dk
        else:
            dv_s[...] += dv
            dk_s[...] += dk

    pipeline([weight_stage, cot_stage, grad_stage], RATIO)
    bg_ref[0] = (dk_s[...] * SCALE).astype(BF)
    bg_ref[1] = dv_s[...].astype(BF)
    done_ref[...] = jnp.zeros_like(done_ref)


def branch_pass(at, count, earlier, q, og, vw, vg, bkv, pieces, stats):
    size, rows = q.shape[0], pieces[0].shape[1]
    plen = YH * X * rows
    operands = [q, og, vw, vg, bkv, *pieces, stats]
    return pl.pallas_call(
        functools.partial(branch_kernel, plen=plen),
        grid=(count,),
        in_specs=common_specs(size, rows, at) + [pl.BlockSpec((1, 3 * RATIO, size), lambda j: (j + at, 0, 0))]
        + [pl.BlockSpec(memory_space=pl.ANY)] * len(earlier),
        out_specs=[pl.BlockSpec((size, RATIO * HD), lambda j: (0, j + at)),
                   pl.BlockSpec((2, size, HD), lambda j: (0, 0, j + at)),
                   pl.BlockSpec((1, KVH * HD), lambda j: (0, 0))],
        out_shape=[jax.ShapeDtypeStruct(q.shape, BF), jax.ShapeDtypeStruct(bkv.shape, BF),
                   jax.ShapeDtypeStruct((1, KVH * HD), F32)],
        scratch_shapes=[
            pltpu.VMEM((plen + size, HD), BF), pltpu.VMEM((plen + size, HD), BF),
            pltpu.VMEM((size, HD), F32), pltpu.VMEM((size, HD), F32), pltpu.VMEM((size, size), F32)],
        input_output_aliases={len(operands) + i: i for i in range(min(2, len(earlier)))},
        compiler_params=pltpu.CompilerParams(vmem_limit_bytes=VMEM),
        cost_estimate=pl.CostEstimate(
            flops=count * 15 * 10**8, bytes_accessed=count * 2 * 10**6, transcendentals=count * 15 * 10**5),
    )(*operands, *earlier)


def my_place():
    return lax.axis_index("z"), lax.axis_index("yl") * CORE + lax.axis_index("c")


def ask_kernel(parents_ref, *refs):
    ring, outs = refs[: Z + 1], refs[Z + 2 :]
    my_z, pair = my_place()
    for t, out in enumerate(outs):
        parent = parents_ref[my_z * FOUR + ((pair + t) & (FOUR - 1))]
        place = (my_z - (parent >> 2)) & (Z - 1)
        for k in range(Z):

            @pl.when(place == k)
            def _():
                if k == Z // 2:
                    out[0] = ring[k][...]
                    out[1] = ring[Z][...]
                else:
                    out[...] = ring[k][...]


def take_kernel(parents_ref, *refs):
    received, out = refs[:FOUR], refs[FOUR]
    my_z, pair = my_place()
    place = (pair - parents_ref[my_z * FOUR + pair]) & (FOUR - 1)
    for k in range(FOUR):

        @pl.when(place == k)
        def _():
            out[...] = received[k][...]


def slot_kernel(parents_ref, *refs):
    ring, outs, acc = refs[: Z + 1], refs[Z + 2 : -1], refs[-1]
    my_z, pair = my_place()
    for t, out in enumerate(outs):
        acc[...] = jnp.zeros_like(acc)
        for k in range(Z):
            parent = parents_ref[((my_z - k) & (Z - 1)) * FOUR + pair]

            @pl.when(parent == my_z * FOUR + ((pair + t) & (FOUR - 1)))
            def _():
                if k == Z // 2:
                    acc[0] += ring[k][...].astype(F32)
                    acc[1] += ring[Z][...].astype(F32)
                else:
                    acc[...] += ring[k][...].astype(F32)

        out[...] = acc[...].astype(out.dtype)


def choose(kernel, parents, blocks, kinds, scratch=(), after=()):
    return pl.pallas_call(
        kernel,
        in_specs=[pl.BlockSpec(memory_space=pltpu.SMEM)] + [pl.BlockSpec(memory_space=pltpu.VMEM)] * len(blocks)
        + [pl.BlockSpec(memory_space=pl.ANY)] * len(after),
        out_specs=[pl.BlockSpec(memory_space=pltpu.VMEM)] * len(kinds),
        out_shape=[jax.ShapeDtypeStruct((2, *blocks[0].shape[-2:]), kind) for kind in kinds],
        scratch_shapes=scratch,
    )(parents, *blocks, *after)


def shift(value, axis, step, size):
    return lax.ppermute(value, axis, [(i, (i + step) % size) for i in range(size)])


def gather_z(value):
    got = {0: value}
    for k in (2, Z - 2, 1, Z - 1):
        got[k] = shift(value, "z", k, Z)
    got[4] = shift(got[2][0], "z", 2, Z)
    got[Z] = shift(got[6][1], "z", -2, Z)
    got[3] = shift(got[2], "z", 1, Z)
    got[5] = shift(got[6], "z", -1, Z)
    return [got[k] for k in range(Z + 1)]


def shards(queries, branch_kv, prefix_kv, out_grad, value_weight, value_grad, parents, lengths):
    own_args = (queries[0, 0], out_grad[0, 0], value_weight[None], value_grad[0], branch_kv[0, 0])
    att, early = early_pass(*own_args)
    asked = choose(ask_kernel, parents, gather_z(prefix_kv[0]), [BF] * FOUR, after=[early])
    received = [asked[0]] + [shift(asked[t], ("yl", "c"), t, FOUR) for t in range(1, FOUR)]
    (picked,) = choose(take_kernel, parents, received, [BF])

    row = [picked] + [shift(picked, "x", k, X) for k in range(1, X)]
    pieces = row + [shift(piece, "yh", 1, YH) for piece in row]

    operands = (*own_args, pieces)
    values, *grads, stats = prefix_pass(lengths[0], *operands, att, early)

    back = grads[:1]
    for i in range(1, YH * X):
        jy, k = divmod(i, X)
        perm = [(b, ((b // X - jy) % YH) * X + (b % X - k) % X) for b in range(YH * X)]
        back.append(lax.ppermute(grads[i], ("yh", "x"), perm))
    *rest, done = branch_pass(0, 1, [], *operands, stats)
    share = (sum(part.astype(F32) for part in back) + done).astype(BF)

    ring = gather_z(share)
    *rest, done = branch_pass(1, 1, [*rest, share], *operands, stats)
    *rest, done = branch_pass(2, 1, [*rest, ring[2]], *operands, stats)
    acc = [pltpu.VMEM(share.shape, F32)]
    own, *others = choose(slot_kernel, parents, ring, [F32, BF, BF, BF], acc, [done])
    query_grad, branch_grad, done = branch_pass(3, 1, [*rest, own], *operands, stats)
    prefix_grad = own + done
    for t in range(1, FOUR):
        prefix_grad += shift(others[t - 1], ("yl", "c"), t, FOUR).astype(F32)
    return values[None], query_grad[None, None], branch_grad[None, None], prefix_grad[None]


def solution(mesh):
    fine = Mesh(mesh.devices.reshape(Z, YL, CORE, YH, X), ("z", "yl", "c", "yh", "x"))
    prefix, branch = ("z", "yl", "c"), ("yh", "x")
    in_specs = (
        P(prefix, branch, None, None),
        P(prefix, branch, None, None, None),
        P(prefix, None, branch, None),
        P(prefix, branch, None, None),
        P(),
        P(prefix, branch, None),
        P(),
        P(prefix, branch),
    )
    out_specs = (
        P(prefix, branch, None),
        P(prefix, branch, None, None),
        P(prefix, branch, None, None, None),
        P(prefix, None, branch, None),
    )
    return jax.shard_map(shards, mesh=fine, in_specs=in_specs, out_specs=out_specs, check_vma=False)
```

```python
import functools

import jax
import jax.numpy as jnp
from jax import lax
from jax.experimental import pallas as pl
from jax.experimental.pallas import tpu as pltpu
from jax.sharding import Mesh, PartitionSpec as P

QH = 32
KVH = 4
HD = 128
RATIO = QH // KVH
LOG2E = 1.4426950408889634
SCALE = HD**-0.5
F32 = jnp.float32
BF = jnp.bfloat16
VMEM = 56 * 1024 * 1024
Z, YL, CORE, YH, X = 8, 2, 2, 2, 4
FOUR = YL * CORE


def tn(a, b):
    return lax.dot_general(a, b, (((0,), (0,)), ((), ())), preferred_element_type=F32)


def nt(a, b):
    return lax.dot_general(a, b, (((1,), (1,)), ((), ())), preferred_element_type=F32)


def nn(a, b):
    return jnp.dot(a, b, preferred_element_type=F32)


def load_keys(k_s, v_s, pieces, bkv_ref, plen, rows):
    for i in range(YH * X):
        k_s[i * rows : (i + 1) * rows, :] = pieces[i][0]
        v_s[i * rows : (i + 1) * rows, :] = pieces[i][1]
    k_s[plen:, :] = bkv_ref[0]
    v_s[plen:, :] = bkv_ref[1]


def set_bias(bias_s):
    size = bias_s.shape[0]
    key_at = lax.broadcasted_iota(jnp.int32, (size, size), 0)
    row_at = lax.broadcasted_iota(jnp.int32, (size, size), 1)
    bias_s[...] = jnp.where(key_at <= row_at, 0.0, -1e30)


def column(row, size):
    return jnp.broadcast_to(row, (8, size)).T[:, :1]


def pipeline(stages, count, late_first=False):
    depth = len(stages)
    order = list(enumerate(stages))
    for step in range(count + depth - 1):
        for late, stage in order[::-1] if late_first else order:
            if 0 <= step - late < count:
                stage(step - late)


def early_kernel(q_ref, og_ref, vw_ref, vg_ref, bkv_ref, att_ref, stat_ref, bias_s):
    size = q_ref.shape[0]

    @pl.when(pl.program_id(0) == 0)
    def _():
        set_bias(bias_s)

    val_t = bkv_ref[1].T
    state = {}

    def score_stage(h):
        s = nt(bkv_ref[0], q_ref[:, h * HD : (h + 1) * HD]) * (SCALE * LOG2E) + bias_s[...]
        top = jnp.max(s, axis=0, keepdims=True)
        p = jnp.exp2(s - top)
        stat_ref[0, h : h + 1, :] = top
        stat_ref[0, RATIO + h : RATIO + h + 1, :] = jnp.sum(p, axis=0, keepdims=True)
        state[h] = p.astype(BF)

    def value_stage(h):
        att_ref[0, h] = nn(val_t, state.pop(h))

    pipeline([score_stage, value_stage], RATIO)


def early_pass(q, og, vw, vg, bkv):
    size = q.shape[0]
    return pl.pallas_call(
        early_kernel,
        grid=(KVH,),
        in_specs=common_specs(size, 0, 0)[:5],
        out_specs=[pl.BlockSpec((1, RATIO, HD, size), lambda j: (j, 0, 0, 0)),
                   pl.BlockSpec((1, 2 * RATIO, size), lambda j: (j, 0, 0))],
        out_shape=[jax.ShapeDtypeStruct((KVH, RATIO, HD, size), F32),
                   jax.ShapeDtypeStruct((KVH, 2 * RATIO, size), F32)],
        scratch_shapes=[pltpu.VMEM((size, size), F32)],
        compiler_params=pltpu.CompilerParams(vmem_limit_bytes=VMEM),
        cost_estimate=pl.CostEstimate(flops=5 * 10**9, bytes_accessed=8 * 10**6, transcendentals=2 * 10**6),
    )(q, og, vw, vg, bkv)


def prefix_kernel(len_ref, q_ref, og_ref, vw_ref, vg_ref, bkv_ref, *rest, plen):
    pieces, att_ref, early_ref = rest[: YH * X], rest[YH * X], rest[YH * X + 1]
    val_ref, *grads, stat_ref, k_s, v_s, dk_s, dv_s, val_s = rest[YH * X + 2 :]
    j = pl.program_id(0)
    size = q_ref.shape[0]
    rows = plen // (YH * X)
    for i in range(YH * X):
        k_s[i * rows : (i + 1) * rows, :] = pieces[i][0]
        v_s[i * rows : (i + 1) * rows, :] = pieces[i][1]
    vg_col = column(vg_ref[...], size)
    live = (lax.broadcasted_iota(jnp.int32, (1, size), 1) < len_ref[0]).astype(F32)
    val_t = v_s[...].T

    @pl.when(j == 0)
    def _():
        val_s[...] = jnp.zeros_like(val_s)

    state = {}
    value_sum = [jnp.zeros((HD, size), F32)]
    vw_cols = jnp.concatenate([vw_ref[:, h * HD : (h + 1) * HD] for h in range(RATIO)], axis=0).T

    def softmax_stage(h):
        cols = slice(h * HD, (h + 1) * HD)
        q = q_ref[:, cols]
        cot = (og_ref[:, cols].astype(F32) + vg_col * vw_ref[:, cols]).astype(BF)
        s = nt(k_s[...], q) * (SCALE * LOG2E)
        early_top = early_ref[0, h : h + 1, :]
        top = jnp.maximum(jnp.max(s, axis=0, keepdims=True), early_top)
        state[h] = (q, cot, s, early_top, top)

    def exp_stage(h):
        q, cot, s, early_top, top = state[h]
        p = jnp.exp2(s - top)
        fade = jnp.exp2(early_top - top)
        total = jnp.sum(p, axis=0, keepdims=True) + fade * early_ref[0, RATIO + h : RATIO + h + 1, :]
        part = live / total
        w = p * part
        stat_ref[0, h : h + 1, :] = top
        stat_ref[0, RATIO + h : RATIO + h + 1, :] = part
        state[h] = (q, cot, w, w.astype(BF), fade * part)

    def cot_stage(h):
        q, cot, w, low, fade = state[h]
        att = nn(val_t, low) + att_ref[0, h] * fade
        dp = nt(v_s[...], cot)
        delta = jnp.sum(cot.T.astype(F32) * att, axis=0, keepdims=True)
        stat_ref[0, 2 * RATIO + h : 2 * RATIO + h + 1, :] = delta
        value_sum[0] = value_sum[0] + att * vw_cols[:, h : h + 1]
        state[h] = (q, cot, w, low, dp, delta)

    def grad_stage(h):
        q, cot, w, low, dp, delta = state.pop(h)
        ds = (w * (dp - delta)).astype(BF)
        dv = nn(low, cot)
        dk = nn(ds, q)
        if h == 0:
            dv_s[...] = dv
            dk_s[...] = dk
        else:
            dv_s[...] += dv
            dk_s[...] += dk

    pipeline([softmax_stage, exp_stage, cot_stage, grad_stage], RATIO, True)
    val_s[...] += value_sum[0]
    dk = (dk_s[...] * SCALE).astype(BF)
    dv = dv_s[...].astype(BF)
    for i in range(YH * X):
        grads[i][0] = dk[i * rows : (i + 1) * rows]
        grads[i][1] = dv[i * rows : (i + 1) * rows]

    @pl.when(j == pl.num_programs(0) - 1)
    def _():
        val_ref[...] = jnp.sum(val_s[...], axis=0, keepdims=True)


def common_specs(size, rows, at):
    wide = RATIO * HD
    return [
        pl.BlockSpec((size, wide), lambda j: (0, j + at)),
        pl.BlockSpec((size, wide), lambda j: (0, j + at)),
        pl.BlockSpec((1, wide), lambda j: (0, j + at)),
        pl.BlockSpec((1, size), lambda j: (0, 0)),
        pl.BlockSpec((2, size, HD), lambda j: (0, 0, j + at)),
    ] + [pl.BlockSpec((2, rows, HD), lambda j: (0, 0, j + at))] * (YH * X)


def prefix_pass(lengths, q, og, vw, vg, bkv, pieces, att, early):
    size, rows = q.shape[0], pieces[0].shape[1]
    plen = YH * X * rows
    grad = jax.ShapeDtypeStruct((2, rows, KVH * HD), BF)
    grad_spec = pl.BlockSpec((2, rows, HD), lambda j: (0, 0, j))
    return pl.pallas_call(
        functools.partial(prefix_kernel, plen=plen),
        grid=(KVH,),
        in_specs=[pl.BlockSpec(memory_space=pltpu.SMEM)] + common_specs(size, rows, 0) + [
            pl.BlockSpec((1, RATIO, HD, size), lambda j: (j, 0, 0, 0)),
            pl.BlockSpec((1, 2 * RATIO, size), lambda j: (j, 0, 0))],
        out_specs=[pl.BlockSpec((1, size), lambda j: (0, 0)), *[grad_spec] * (YH * X),
                   pl.BlockSpec((1, 3 * RATIO, size), lambda j: (j, 0, 0))],
        out_shape=[jax.ShapeDtypeStruct((1, size), F32), *[grad] * (YH * X),
                   jax.ShapeDtypeStruct((KVH, 3 * RATIO, size), F32)],
        scratch_shapes=[
            pltpu.VMEM((plen, HD), BF), pltpu.VMEM((plen, HD), BF),
            pltpu.VMEM((plen, HD), F32), pltpu.VMEM((plen, HD), F32),
            pltpu.VMEM((HD, size), F32)],
        compiler_params=pltpu.CompilerParams(vmem_limit_bytes=VMEM),
        cost_estimate=pl.CostEstimate(flops=8 * 10**9, bytes_accessed=8 * 10**6, transcendentals=6 * 10**6),
    )(lengths, q, og, vw, vg, bkv, *pieces, att, early)


def branch_kernel(q_ref, og_ref, vw_ref, vg_ref, bkv_ref, *rest, plen):
    pieces, stat_ref = rest[: YH * X], rest[YH * X]
    dq_ref, bg_ref, done_ref, k_s, v_s, dk_s, dv_s, bias_s = rest[-8:]
    size = q_ref.shape[0]
    rows = plen // (YH * X)
    load_keys(k_s, v_s, pieces, bkv_ref, plen, rows)
    vg_col = column(vg_ref[...], size)
    set_bias(bias_s)
    state = {}

    def weight_stage(h):
        cols = slice(h * HD, (h + 1) * HD)
        q = q_ref[:, cols]
        cot = (og_ref[:, cols].astype(F32) + vg_col * vw_ref[:, cols]).astype(BF)
        s = nt(k_s[...], q)
        top = stat_ref[0, h : h + 1, :]
        part = stat_ref[0, RATIO + h : RATIO + h + 1, :]
        wp = jnp.exp2(s[:plen] * (SCALE * LOG2E) - top) * part
        wb = jnp.exp2(s[plen:] * (SCALE * LOG2E) + bias_s[...] - top) * part
        state[h] = (q, cot, wp, wb)

    def cot_stage(h):
        q, cot, wp, wb = state[h]
        delta = stat_ref[0, 2 * RATIO + h : 2 * RATIO + h + 1, :]
        dp = nt(v_s[...], cot)
        ds = jnp.concatenate([(wp * (dp[:plen] - delta)).astype(BF), (wb * (dp[plen:] - delta)).astype(BF)], axis=0)
        state[h] = (q, cot, wb.astype(BF), ds)

    def grad_stage(h):
        q, cot, low, ds = state.pop(h)
        dq_ref[:, h * HD : (h + 1) * HD] = (tn(ds, k_s[...]) * SCALE).astype(BF)
        dv = nn(low, cot)
        dk = nn(ds[plen:], q)
        if h == 0:
            dv_s[...] = dv
            dk_s[...] = dk
        else:
            dv_s[...] += dv
            dk_s[...] += dk

    pipeline([weight_stage, cot_stage, grad_stage], RATIO)
    bg_ref[0] = (dk_s[...] * SCALE).astype(BF)
    bg_ref[1] = dv_s[...].astype(BF)
    done_ref[...] = jnp.zeros_like(done_ref)


def branch_pass(at, count, earlier, q, og, vw, vg, bkv, pieces, stats):
    size, rows = q.shape[0], pieces[0].shape[1]
    plen = YH * X * rows
    operands = [q, og, vw, vg, bkv, *pieces, stats]
    return pl.pallas_call(
        functools.partial(branch_kernel, plen=plen),
        grid=(count,),
        in_specs=common_specs(size, rows, at) + [pl.BlockSpec((1, 3 * RATIO, size), lambda j: (j + at, 0, 0))]
        + [pl.BlockSpec(memory_space=pl.ANY)] * len(earlier),
        out_specs=[pl.BlockSpec((size, RATIO * HD), lambda j: (0, j + at)),
                   pl.BlockSpec((2, size, HD), lambda j: (0, 0, j + at)),
                   pl.BlockSpec((1, KVH * HD), lambda j: (0, 0))],
        out_shape=[jax.ShapeDtypeStruct(q.shape, BF), jax.ShapeDtypeStruct(bkv.shape, BF),
                   jax.ShapeDtypeStruct((1, KVH * HD), F32)],
        scratch_shapes=[
            pltpu.VMEM((plen + size, HD), BF), pltpu.VMEM((plen + size, HD), BF),
            pltpu.VMEM((size, HD), F32), pltpu.VMEM((size, HD), F32), pltpu.VMEM((size, size), F32)],
        input_output_aliases={len(operands) + i: i for i in range(min(2, len(earlier)))},
        compiler_params=pltpu.CompilerParams(vmem_limit_bytes=VMEM),
        cost_estimate=pl.CostEstimate(
            flops=count * 15 * 10**8, bytes_accessed=count * 2 * 10**6, transcendentals=count * 15 * 10**5),
    )(*operands, *earlier)


def my_place():
    return lax.axis_index("z"), lax.axis_index("yl") * CORE + lax.axis_index("c")


def ask_kernel(parents_ref, *refs):
    ring, outs = refs[:Z], refs[Z + 1 :]
    my_z, pair = my_place()
    for t, out in enumerate(outs):
        parent = parents_ref[my_z * FOUR + ((pair + t) & (FOUR - 1))]
        place = (my_z - (parent >> 2)) & (Z - 1)
        for k in range(Z):

            @pl.when(place == k)
            def _():
                out[...] = ring[k][...]


def take_kernel(parents_ref, *refs):
    received, out = refs[:FOUR], refs[FOUR]
    my_z, pair = my_place()
    place = (pair - parents_ref[my_z * FOUR + pair]) & (FOUR - 1)
    for k in range(FOUR):

        @pl.when(place == k)
        def _():
            out[...] = received[k][...]


def slot_kernel(parents_ref, *refs):
    ring, outs, acc = refs[:Z], refs[Z + 1 : -1], refs[-1]
    my_z, pair = my_place()
    for t, out in enumerate(outs):
        acc[...] = jnp.zeros_like(acc)
        for k in range(Z):
            parent = parents_ref[((my_z - k) & (Z - 1)) * FOUR + pair]

            @pl.when(parent == my_z * FOUR + ((pair + t) & (FOUR - 1)))
            def _():
                acc[...] += ring[k][...].astype(F32)

        out[...] = acc[...].astype(out.dtype)


def choose(kernel, parents, blocks, kinds, scratch=(), after=()):
    return pl.pallas_call(
        kernel,
        in_specs=[pl.BlockSpec(memory_space=pltpu.SMEM)] + [pl.BlockSpec(memory_space=pltpu.VMEM)] * len(blocks)
        + [pl.BlockSpec(memory_space=pl.ANY)] * len(after),
        out_specs=[pl.BlockSpec(memory_space=pltpu.VMEM)] * len(kinds),
        out_shape=[jax.ShapeDtypeStruct((2, *blocks[0].shape[-2:]), kind) for kind in kinds],
        scratch_shapes=scratch,
    )(parents, *blocks, *after)


def shift(value, axis, step, size):
    return lax.ppermute(value, axis, [(i, (i + step) % size) for i in range(size)])


def gather_z(value):
    got = {0: value}
    for k in (2, Z - 2, 1, Z - 1):
        got[k] = shift(value, "z", k, Z)
    got[4] = shift(got[2], "z", 2, Z)
    got[3] = shift(got[2], "z", 1, Z)
    got[5] = shift(got[6], "z", -1, Z)
    return [got[k] for k in range(Z)]


def shards(queries, branch_kv, prefix_kv, out_grad, value_weight, value_grad, parents, lengths):
    own_args = (queries[0, 0], out_grad[0, 0], value_weight[None], value_grad[0], branch_kv[0, 0])
    att, early = early_pass(*own_args)
    asked = choose(ask_kernel, parents, gather_z(prefix_kv[0]), [BF] * FOUR, after=[early])
    received = [asked[0]] + [shift(asked[t], ("yl", "c"), t, FOUR) for t in range(1, FOUR)]
    (picked,) = choose(take_kernel, parents, received, [BF])

    row = [picked] + [shift(picked, "x", k, X) for k in range(1, X)]
    pieces = row + [shift(piece, "yh", 1, YH) for piece in row]

    operands = (*own_args, pieces)
    values, *grads, stats = prefix_pass(lengths[0], *operands, att, early)

    back = grads[:1]
    for i in range(1, YH * X):
        jy, k = divmod(i, X)
        perm = [(b, ((b // X - jy) % YH) * X + (b % X - k) % X) for b in range(YH * X)]
        back.append(lax.ppermute(grads[i], ("yh", "x"), perm))
    *rest, done = branch_pass(0, 1, [], *operands, stats)
    share = (sum(part.astype(F32) for part in back) + done).astype(BF)

    ring = gather_z(share)
    *rest, done = branch_pass(1, 1, [*rest, share], *operands, stats)
    *rest, done = branch_pass(2, 1, [*rest, ring[2]], *operands, stats)
    acc = [pltpu.VMEM(share.shape, F32)]
    own, *others = choose(slot_kernel, parents, ring, [F32, BF, BF, BF], acc, [done])
    query_grad, branch_grad, done = branch_pass(3, 1, [*rest, own], *operands, stats)
    prefix_grad = own + done
    for t in range(1, FOUR):
        prefix_grad += shift(others[t - 1], ("yl", "c"), t, FOUR).astype(F32)
    return values[None], query_grad[None, None], branch_grad[None, None], prefix_grad[None]


def solution(mesh):
    fine = Mesh(mesh.devices.reshape(Z, YL, CORE, YH, X), ("z", "yl", "c", "yh", "x"))
    prefix, branch = ("z", "yl", "c"), ("yh", "x")
    in_specs = (
        P(prefix, branch, None, None),
        P(prefix, branch, None, None, None),
        P(prefix, None, branch, None),
        P(prefix, branch, None, None),
        P(),
        P(prefix, branch, None),
        P(),
        P(prefix, branch),
    )
    out_specs = (
        P(prefix, branch, None),
        P(prefix, branch, None, None),
        P(prefix, branch, None, None, None),
        P(prefix, None, branch, None),
    )
    return jax.shard_map(shards, mesh=fine, in_specs=in_specs, out_specs=out_specs, check_vma=False)
```
